512 devices in a mesh: layer: 4 (over y), row: 4 (over x), col: 32 (over z, core).
Axes of the slice: x: 4, y: 4, z: 16, core: 2. Of those that a mesh axis runs over, the one named last changes fastest.
Arguments:
- leaf_rhs: bfloat16 [1024, 128, 256], P(('layer', 'row', 'col')), may hold values from -6 to 6
- leaf_lower_inv: bfloat16 [1024, 128, 128], P(('layer', 'row', 'col'))
- leaf_upper_inv: bfloat16 [1024, 128, 128], P(('layer', 'row', 'col'))
- leaf_lower: bfloat16 [1024, 4, 128, 128], P(('layer', 'row', 'col')), may hold values from -0.125 to 0.125
- leaf_upper: bfloat16 [1024, 4, 128, 128], P(('layer', 'row', 'col')), may hold values from -0.25 to 0.25
- targets: int32 [1024, 4], P(('layer', 'row', 'col')), may hold values from 0 to 63, as said below
- sep_rhs: float32 [256, 128, 256], P(('row', 'col')), may hold values from -6 to 6
- sep_lower_inv: float32 [256, 128, 128], P(('row', 'col')), as said below
- sep_upper_inv: float32 [256, 128, 128], P(('row', 'col')), as said below
- sep_lower_link: float32 [256, 128, 128], P(('row', 'col'))
- sep_upper_link: float32 [256, 128, 128], P(('row', 'col'))
Outputs:
- leaf_solution: bfloat16 [1024, 128, 256], P(('layer', 'row', 'col'))
- sep_solution: float32 [256, 128, 256], P(('row', 'col'))
The draws below stay inside these ranges and needn't reach their ends.
Inputs may be any that keep to these rules, and one draw needn't show every extreme that they name: Each leaf names 4 different separators of its own grid row; separators t and u with t // 2 == u // 2 are owned by the same col index, and among the targets of one device's 2 leaves at most one separator of each such owner appears. `sep_lower_inv`: diagonally dominant blocks. `sep_upper_inv`: diagonally dominant blocks.
All inputs are finite; a program needn't handle non-finite values.
Results may differ from the reference program's by a relative error of at most 0.007.
Values may be sent and summed in bfloat16 or wider, within the bound.
No kernel may reach another device: no remote copies, remote signals or barrier semaphores. Data moves between devices by JAX's collectives and lax.ppermute only.
A program may use at most 128 MiB of HBM per device.

```python
import math
import jax
import jax.numpy as jnp
from jax import lax

B = 128
RHS = 256
LEAF_DEV = 2
UPD = 4
SEP_DEV = 2
LEAVES = 1024
SEPS = 256
N_LAYER = 4
N_ROW = 4
N_COL = 32


def dominant_blocks(key, count, spread, off_scale):
    key_diag, key_off = jax.random.split(key)
    diagonal = jnp.exp(jax.random.uniform(key_diag, (count, B), jnp.float32, -spread, spread))
    off_part = jax.random.normal(key_off, (count, B, B), jnp.float32)
    identity = jnp.eye(B, dtype=jnp.float32)[None]
    return diagonal[:, :, None] * identity + off_scale * off_part / math.sqrt(B)


def chain_links(key):
    key_rate, key_jitter, key_off = jax.random.split(key, 3)
    decays = jnp.exp(jax.random.uniform(key_rate, (B,), jnp.float32, math.log(0.25), math.log(64.0)))
    jitter = jnp.exp(jax.random.uniform(key_jitter, (SEPS, B), jnp.float32, -0.35, 0.35))
    keeping = jnp.exp(-decays[None, :] * jitter / SEPS)
    off_part = jax.random.normal(key_off, (SEPS, B, B), jnp.float32)
    identity = jnp.eye(B, dtype=jnp.float32)[None]
    return -keeping[:, :, None] * identity + 0.05 * off_part / math.sqrt(B)


def draw_targets(key, part):
    key = jax.random.fold_in(key, 15)
    key_pop, key_noise, key_bits = jax.random.split(key, 3)
    device_total = LEAVES // LEAF_DEV
    popular = jax.random.randint(key_pop, (N_COL,), 0, 2048, dtype=jnp.int32)
    noise = jax.random.randint(key_noise, (LEAVES, N_COL), 0, 1024, dtype=jnp.int32)
    owner_ids = jnp.arange(N_COL, dtype=jnp.int32)[None, :]
    leaf_ids = jnp.arange(LEAVES, dtype=jnp.int32)[:, None]
    forced = jnp.where((leaf_ids == 0) & ((owner_ids == 0) | (owner_ids == N_COL - 1)), 4096, 0)
    scores = (noise + popular[None, :] + forced) * N_COL + owner_ids
    unused, owners = lax.top_k(scores, UPD)
    bits = jax.random.randint(key_bits, (device_total, N_COL), 0, SEP_DEV, dtype=jnp.int32)
    device_ids = jnp.arange(device_total, dtype=jnp.int32)[:, None]
    bits = jnp.where((device_ids == 0) & (owner_ids == 0), 0, bits)
    bits = jnp.where((device_ids == 0) & (owner_ids == N_COL - 1), SEP_DEV - 1, bits)
    leaf_bits = bits[jnp.arange(LEAVES, dtype=jnp.int32) // LEAF_DEV]
    chosen = jnp.take_along_axis(leaf_bits, owners, axis=1)
    return (owners * SEP_DEV + chosen).astype(jnp.int32)


def draw_leaf_lower_inv(key, part):
    key = jax.random.fold_in(key, 3)
    return dominant_blocks(key, LEAVES, 0.7, 0.3).astype(jnp.bfloat16)


def draw_leaf_upper_inv(key, part):
    key = jax.random.fold_in(key, 5)
    return dominant_blocks(key, LEAVES, 0.7, 0.3).astype(jnp.bfloat16)


def draw_sep_lower_inv(key, part):
    key = jax.random.fold_in(key, 7)
    return dominant_blocks(key, SEPS, 0.02, 0.05)


def draw_sep_upper_inv(key, part):
    key = jax.random.fold_in(key, 9)
    return dominant_blocks(key, SEPS, 0.02, 0.05)


def draw_sep_lower_link(key, part):
    key = jax.random.fold_in(key, 11)
    return chain_links(key)


def draw_sep_upper_link(key, part):
    key = jax.random.fold_in(key, 13)
    return chain_links(key)


def shard_levels(rng, extent, cuts, smallest, high):
    level = 1.0
    for position, shards_of in cuts:
        steps = jax.random.uniform(jax.random.fold_in(jax.random.fold_in(rng, 6), position), (shards_of,), jnp.float32, smallest / len(cuts), high / len(cuts))
        level = level * jnp.repeat(jnp.exp(steps), extent[position] // shards_of).reshape((-1,) + (1,) * (len(extent) - 1 - position))
    return level


def gaussian(stream_key, dims, deviation, bound, cuts=(), held_as=jnp.bfloat16):
    entries = jax.random.normal(stream_key, dims, jnp.float32) * deviation
    if len(cuts) > 0:
        entries = shard_levels(stream_key, dims, cuts, -0.22, 0.18) * entries
    return jnp.clip(entries, min=-bound, max=bound).astype(held_as)


def setup_inputs(seed: int = 0) -> dict:
    key_list = jax.random.split(jax.random.key(seed), 12)
    leaf_rhs = gaussian(key_list[0], (LEAVES, B, RHS), 1.0, 6.0, ((0, 512),))
    leaf_lower_inv = draw_leaf_lower_inv(jax.random.fold_in(key_list[11], 71), 0)
    leaf_upper_inv = draw_leaf_upper_inv(jax.random.fold_in(key_list[11], 71), 0)
    leaf_lower = gaussian(key_list[3], (LEAVES, UPD, B, B), (B * N_LAYER * LEAF_DEV * UPD // SEP_DEV) ** -0.5, 0.125, ((0, 512),))
    leaf_upper = gaussian(key_list[4], (LEAVES, UPD, B, B), (B * UPD) ** -0.5, 0.25, ((0, 512),))
    targets = draw_targets(jax.random.fold_in(key_list[11], 71), 0)
    sep_rhs = gaussian(key_list[6], (SEPS, B, RHS), 1.0, 6.0, ((0, 128),), jnp.float32)
    sep_lower_inv = draw_sep_lower_inv(jax.random.fold_in(key_list[11], 71), 0)
    sep_upper_inv = draw_sep_upper_inv(jax.random.fold_in(key_list[11], 71), 0)
    sep_lower_link = draw_sep_lower_link(jax.random.fold_in(key_list[11], 71), 0)
    sep_upper_link = draw_sep_upper_link(jax.random.fold_in(key_list[11], 71), 0)
    return dict(leaf_rhs=leaf_rhs, leaf_lower_inv=leaf_lower_inv, leaf_upper_inv=leaf_upper_inv, leaf_lower=leaf_lower, leaf_upper=leaf_upper, targets=targets, sep_rhs=sep_rhs, sep_lower_inv=sep_lower_inv, sep_upper_inv=sep_upper_inv, sep_lower_link=sep_lower_link, sep_upper_link=sep_upper_link)


highest = lax.Precision.HIGHEST


def reference(leaf_rhs, leaf_lower_inv, leaf_upper_inv, leaf_lower, leaf_upper, targets, sep_rhs, sep_lower_inv, sep_upper_inv, sep_lower_link, sep_upper_link):
    row_seps = SEP_DEV * N_COL
    device_total = LEAVES // LEAF_DEV

    def per_device(array):
        return array.reshape((device_total, LEAF_DEV) + array.shape[1:])

    device_ids = jnp.arange(device_total, dtype=jnp.int32)

    def row_offset(device):
        return ((device // N_COL) % N_ROW * row_seps).astype(jnp.int32)

    def forward_device(running, inputs):
        rhs_block, inverse, lower, chosen, device = inputs
        forward_leaf = jnp.einsum('kab,kbr->kar', inverse.astype(jnp.float32), rhs_block.astype(jnp.float32)).astype(jnp.bfloat16)
        updates = jnp.einsum('kiab,kbr->kiar', lower.astype(jnp.float32), forward_leaf.astype(jnp.float32))
        onehot = (chosen[:, :, None] == jnp.arange(row_seps, dtype=jnp.int32)[None, None, :]).astype(jnp.float32)
        partial_value = jnp.einsum('kis,kiar->sar', onehot, updates, precision=highest).astype(jnp.bfloat16)
        offset = row_offset(device)
        current = lax.dynamic_slice_in_dim(running, offset, row_seps, 0)
        running = lax.dynamic_update_slice_in_dim(running, current + partial_value.astype(jnp.float32), offset, 0)
        return running, forward_leaf

    totals, forward_all = lax.scan(forward_device, jnp.zeros((SEPS, B, RHS), jnp.float32),
                                   (per_device(leaf_rhs), per_device(leaf_lower_inv), per_device(leaf_lower), per_device(targets), device_ids))
    chain_rhs = sep_rhs - totals

    def chain_step(previous, inputs):
        inverse, link, right = inputs
        current = jnp.dot(inverse, right - jnp.dot(link, previous, precision=highest), precision=highest)
        return current, current

    start_zero = jnp.zeros((B, RHS), jnp.float32)
    final_down, chain_fwd = lax.scan(chain_step, start_zero, (sep_lower_inv, sep_lower_link, chain_rhs))
    final_up, sep_solution = lax.scan(chain_step, start_zero, (sep_upper_inv, sep_upper_link, chain_fwd), reverse=True)
    solved_low = sep_solution.astype(jnp.bfloat16)

    def backward_device(inputs):
        forward_leaf, inverse, upper, chosen, device = inputs
        row_block = lax.dynamic_slice_in_dim(solved_low, row_offset(device), row_seps, 0)
        picked = row_block[chosen]
        updates = jnp.einsum('kiab,kibr->kar', upper.astype(jnp.float32), picked.astype(jnp.float32))
        residual = (forward_leaf.astype(jnp.float32) - updates).astype(jnp.bfloat16)
        return jnp.einsum('kab,kbr->kar', inverse.astype(jnp.float32), residual.astype(jnp.float32)).astype(jnp.bfloat16)

    leaf_solution = lax.map(backward_device, (forward_all, per_device(leaf_upper_inv), per_device(leaf_upper), per_device(targets), device_ids))
    return leaf_solution.reshape(LEAVES, B, RHS), sep_solution
```

```python
import jax
import jax.numpy as jnp
from jax import lax
from jax.experimental import pallas as pl
from jax.experimental.pallas import tpu as pltpu
from jax.sharding import Mesh
from jax.sharding import PartitionSpec as P

f32 = jnp.float32
bf16 = jnp.bfloat16

B = 128
VMEM_LIMIT = 40 * 1024 * 1024


def dot(a, b):
    return jnp.dot(a, b, preferred_element_type=f32)


def dot_nt(a, b):
    return lax.dot_general(a, b, (((1,), (1,)), ((), ())), preferred_element_type=f32)


def split(x):
    high = x.astype(bf16)
    return high, (x - high.astype(f32)).astype(bf16)


def mm(a, b):
    a_high, a_low = split(a)
    b_high, b_low = split(b)
    return dot(a_high, b_high) + (dot(a_low, b_high) + dot(a_high, b_low))


def call(kernel, outs, scratch=(), name=None, smem=()):
    def run(*operands):
        return pl.pallas_call(
            kernel,
            out_shape=outs,
            in_specs=[
                pl.BlockSpec(memory_space=pltpu.SMEM if k in smem else pltpu.VMEM)
                for k in range(len(operands))
            ],
            out_specs=jax.tree.map(lambda _: pl.BlockSpec(memory_space=pltpu.VMEM), outs),
            scratch_shapes=list(scratch),
            compiler_params=pltpu.CompilerParams(vmem_limit_bytes=VMEM_LIMIT),
            name=name,
        )(*operands)

    return run


def shaped(shape, dtype):
    return jax.ShapeDtypeStruct(shape, dtype)


def leaf_forward(rhs_ref, inv_ref, lower_ref, tgt_ref, out_ref):
    groups, width = out_ref.shape[0], 256 // out_ref.shape[0]
    for k in range(2):
        forward = dot(inv_ref[k], rhs_ref[k]).T.astype(bf16)
        for j in range(groups):
            out_ref[j, (8 + k) * width : (9 + k) * width] = forward[j * width : (j + 1) * width]
        for i in range(4):
            update = dot_nt(forward, lower_ref[k, i]).astype(bf16)
            slot = 4 * k + i
            for j in range(groups):
                out_ref[j, slot * width : (slot + 1) * width] = update[j * width : (j + 1) * width]
    for j in range(groups):
        out_ref[j, 10 * width :] = tgt_ref[...]


def scatter_updates(place_ref, got_ref, out_ref, total):
    width = out_ref.shape[-2]
    total[...] = jnp.zeros_like(total)
    for j in range(got_ref.shape[0]):
        for slot in range(8):
            s = place_ref[j, slot]
            total[s] = total[s] + got_ref[j, slot * width : (slot + 1) * width].astype(f32)
    out_ref[...] = total[...].reshape(out_ref.shape).astype(bf16)


def sep_prepare(at_ref, rhs_ref, li_ref, ll_ref, ui_ref, ul_ref, out_ref, turned):
    width = out_ref.shape[2] - 4 * B
    for s in range(2):
        turned[s] = rhs_ref[s].T
        li, ui = li_ref[s], ui_ref[s]
        blocks = (-mm(li, ll_ref[s]).T, -mm(ui, ul_ref[s]).T, li.T, ui.T)
        for c in range(2):
            for k in range(4):
                out_ref[c, s, k * B : (k + 1) * B] = blocks[k]
            first = pl.multiple_of((2 * at_ref[0] + c) * width, width)
            out_ref[c, s, 4 * B :] = turned[s, pl.ds(first, width)]


def chip_maps(sep_ref, pqr_ref, wy_ref):
    def block(s, k):
        return sep_ref[s // 2, s % 2, k * B : (k + 1) * B]

    reach = [block(0, 0)]
    for s in range(1, 4):
        reach.append(mm(reach[-1], block(s, 0)))
    w = mm(reach[3], block(3, 3))
    y = block(3, 1)
    wy = jnp.concatenate([w, y], axis=0)
    wy_ref[:, 3 * B :] = wy
    for s in (2, 1, 0):
        wy = mm(wy, block(s, 1))
        wy = jnp.concatenate([wy[:B] + mm(reach[s], block(s, 3)), wy[B:]], axis=0)
        wy_ref[:, s * B : (s + 1) * B] = wy
    for n in range(pqr_ref.shape[0]):
        pqr_ref[n, 0] = reach[3]
        pqr_ref[n, 1] = wy[B:]
        pqr_ref[n, 2] = wy[:B]


def chip_solve(got_ref, sep_ref, bg_ref, local_ref):
    total = jnp.sum(got_ref[...].astype(f32), axis=0)

    def block(s, k):
        return sep_ref[s // 2, s % 2, k * B : (k + 1) * B]

    base = [
        mm(sep_ref[s // 2, s % 2, 4 * B :] - total[s], block(s, 2)) for s in range(4)
    ]
    f = base[0]
    forward = [f]
    for s in range(1, 4):
        f = mm(f, block(s, 0)) + base[s]
        forward.append(f)
    bent = [mm(forward[s], block(s, 3)) for s in range(4)]
    u = bent[3]
    local_ref[3] = u
    for s in (2, 1, 0):
        u = mm(u, block(s, 1)) + bent[s]
        local_ref[s] = u
    for n in range(bg_ref.shape[0]):
        bg_ref[n, 0] = f
        bg_ref[n, 1] = u


def level_maps(axis):
    def kernel(at_ref, maps_ref, pqr_ref, xyz_ref, keep):
        count = maps_ref.shape[0]
        identity = (
            lax.broadcasted_iota(jnp.int32, (B, B), 0) == lax.broadcasted_iota(jnp.int32, (B, B), 1)
        ).astype(f32)
        x = identity
        keep[0, 0] = x
        xs = [x]
        for q in range(count):
            x = maps_ref[0, 0] if q == 0 else mm(x, maps_ref[q, 0])
            xs.append(x)
            if q + 1 < count:
                keep[q + 1, 0] = x
        zy = jnp.concatenate([jnp.zeros((B, B), f32), identity], axis=0)
        for q in reversed(range(count)):
            keep[q, 1] = zy[B:]
            keep[q, 2] = zy[:B]
            if q == count - 1:
                zy = jnp.concatenate([mm(xs[q], maps_ref[q, 2]), maps_ref[q, 1]], axis=0)
            else:
                turned = maps_ref[0, 2] if q == 0 else mm(xs[q], maps_ref[q, 2])
                zy = mm(zy, maps_ref[q, 1])
                zy = jnp.concatenate([zy[:B] + turned, zy[B:]], axis=0)
        xyz_ref[...] = keep[at_ref[axis]]
        for n in range(pqr_ref.shape[0]):
            pqr_ref[n, 0] = xs[count]
            pqr_ref[n, 1] = zy[B:]
            pqr_ref[n, 2] = zy[:B]

    return kernel


def level_chain(maps_ref, bg_ref, keep):
    count = maps_ref.shape[0]
    f = jnp.zeros(bg_ref.shape[2:], f32)
    entering = []
    for q in range(count):
        keep[q, 0] = f
        entering.append(f)
        f = bg_ref[0, 0] if q == 0 else mm(f, maps_ref[q, 0]) + bg_ref[q, 0]
    u = jnp.zeros_like(f)
    for q in reversed(range(count)):
        keep[q, 1] = u
        turned = bg_ref[q, 1]
        if q > 0:
            turned = turned + mm(entering[q], maps_ref[q, 2])
        u = turned if q == count - 1 else mm(u, maps_ref[q, 1]) + turned
    return f, u


def level_solve(axis):
    def kernel(at_ref, maps_ref, bg_ref, out_ref, own_ref, keep):
        f, u = level_chain(maps_ref, bg_ref, keep)
        own_ref[...] = keep[at_ref[axis]]
        for n in range(out_ref.shape[0]):
            out_ref[n, 0] = f
            out_ref[n, 1] = u

    return kernel


def top_solve(at_ref, maps_ref, bg_ref, xyz_hi_ref, own_hi_ref, xyz_lo_ref, own_lo_ref, wy_ref, local_ref,
              sep_ref, low_ref, keep):
    level_chain(maps_ref, bg_ref, keep)
    place = at_ref[3]
    f, u = keep[place, 0], keep[place, 1]
    for xyz, own in ((xyz_hi_ref, own_hi_ref), (xyz_lo_ref, own_lo_ref)):
        f, u = (
            mm(f, xyz[0]) + own[0],
            mm(u, xyz[1]) + mm(f, xyz[2]) + own[1],
        )
    reached = mm(jnp.concatenate([f, u], axis=1), wy_ref[...])
    for s in range(4):
        value = local_ref[s] + reached[:, s * B : (s + 1) * B]
        for n in range(sep_ref.shape[0] // 2):
            sep_ref[2 * n + s // 2, s % 2] = value
        low = value.astype(bf16)
        for n in range(low_ref.shape[0]):
            low_ref[n, s] = low


def leaf_backward(place_ref, solved_ref, got_ref, upper_ref, inv_ref, out_ref):
    width = out_ref.shape[2]
    for j in range(out_ref.shape[0]):
        for k in range(2):
            total = jnp.zeros((width, B), f32)
            for i in range(4):
                total = total + dot_nt(solved_ref[place_ref[j, 4 * k + i]], upper_ref[j, k, i])
            forward = got_ref[j, (8 + k) * width : (9 + k) * width].astype(f32)
            out_ref[j, k] = dot_nt((forward - total).astype(bf16), inv_ref[j, k]).astype(bf16)


def turn_back(got_ref, out_ref):
    width = got_ref.shape[2]
    for s in range(out_ref.shape[0]):
        for j in range(got_ref.shape[0]):
            part = got_ref[j, s].astype(f32)
            out_ref[s, :, j * width : (j + 1) * width] = part.T.astype(out_ref.dtype)


def exchange(value, axes):
    return lax.all_to_all(value, axes, split_axis=0, concat_axis=0, tiled=True)


def on_device(
    leaf_rhs,
    leaf_lower_inv,
    leaf_upper_inv,
    leaf_lower,
    leaf_upper,
    targets,
    sep_rhs,
    sep_lower_inv,
    sep_upper_inv,
    sep_lower_link,
    sep_upper_link,
):
    across = ("layer", "core")
    layers, rows = lax.axis_size("layer"), lax.axis_size("row")
    highs, lows = lax.axis_size("zh"), lax.axis_size("zl")
    groups = 2 * layers
    width = 256 // groups
    chips = highs * lows
    at = jnp.stack(
        [lax.axis_index(name) for name in ("layer", "zl", "zh", "row")]
    ).astype(jnp.int32)

    mine = call(
        sep_prepare,
        shaped((2, 2, 4 * B + width, B), f32),
        [pltpu.VMEM((2, 256, B), f32)],
        "sep_prepare",
        (0,),
    )(at, sep_rhs, sep_lower_inv, sep_lower_link, sep_upper_inv, sep_upper_link)
    seps = exchange(mine, "core")
    pqr, wy = call(
        chip_maps,
        (shaped((lows, 3, B, B), f32), shaped((2 * B, 4 * B), f32)),
        name="chip_maps",
    )(seps)

    sent_targets = jnp.zeros((16, B), bf16).at[0, :8].set(targets.reshape(8).astype(bf16))
    sent = call(
        leaf_forward, shaped((groups, 10 * width + 16, B), bf16), name="leaf_forward"
    )(leaf_rhs, leaf_lower_inv, leaf_lower, sent_targets)
    upper = lax.all_gather(leaf_upper, across)
    upper_inv = lax.all_gather(leaf_upper_inv, across)
    got = exchange(sent, across)
    place = got[:, 10 * width, :8].astype(jnp.int32)
    sums = call(
        scatter_updates,
        shaped((chips, 4, width, B), bf16),
        [pltpu.VMEM((4 * chips, width, B), f32)],
        "scatter_updates",
        (0,),
    )(place, got)

    lo_maps = exchange(pqr, "zl")
    pqr_hi, xyz_lo = call(
        level_maps(1),
        (shaped((highs, 3, B, B), f32), shaped((3, B, B), f32)),
        [pltpu.VMEM((lows, 3, B, B), f32)],
        "maps_lo",
        (0,),
    )(at, lo_maps)
    hi_maps = exchange(pqr_hi, "zh")
    pqr_top, xyz_hi = call(
        level_maps(2),
        (shaped((rows, 3, B, B), f32), shaped((3, B, B), f32)),
        [pltpu.VMEM((highs, 3, B, B), f32)],
        "maps_hi",
        (0,),
    )(at, hi_maps)
    top_maps = exchange(pqr_top, "row")

    summed = exchange(sums, ("zh", "zl"))
    pair = (2, width, B)
    bg, local = call(
        chip_solve,
        (shaped((lows,) + pair, f32), shaped((4, width, B), f32)),
        name="chip_solve",
    )(summed, seps)
    bg, own_lo = call(
        level_solve(1),
        (shaped((highs,) + pair, f32), shaped(pair, f32)),
        [pltpu.VMEM((lows,) + pair, f32)],
        "solve_lo",
        (0,),
    )(at, lo_maps, exchange(bg, "zl"))
    bg, own_hi = call(
        level_solve(2),
        (shaped((rows,) + pair, f32), shaped(pair, f32)),
        [pltpu.VMEM((highs,) + pair, f32)],
        "solve_hi",
        (0,),
    )(at, hi_maps, exchange(bg, "zh"))
    solved, solved_low = call(
        top_solve,
        (shaped((groups, 2, width, B), f32), shaped((chips, 4, width, B), bf16)),
        [pltpu.VMEM((rows,) + pair, f32)],
        "top_solve",
        (0,),
    )(at, top_maps, exchange(bg, "row"), xyz_hi, own_hi, xyz_lo, own_lo, wy, local)

    low = exchange(solved_low, ("zh", "zl")).reshape(4 * chips, width, B)
    sep_part = call(turn_back, shaped((2, B, 256), f32), name="turn_sep")(exchange(solved, across))
    back = call(
        leaf_backward, shaped((groups, 2, width, B), bf16), name="leaf_backward", smem=(0,)
    )(place, low, got, upper, upper_inv)
    leaf_part = call(turn_back, shaped((2, B, 256), bf16), name="turn_leaf")(exchange(back, across))
    return (leaf_part, sep_part)


def solution(mesh):
    layers, rows, cols = (mesh.shape[name] for name in ("layer", "row", "col"))
    lows = 4
    fine = Mesh(
        mesh.devices.reshape(layers, rows, cols // (2 * lows), lows, 2),
        ("layer", "row", "zh", "zl", "core"),
    )
    leaf = ("layer", "row", "zh", "zl", "core")
    sep = ("row", "zh", "zl", "core")
    return jax.shard_map(
        on_device,
        mesh=fine,
        in_specs=(P(leaf),) * 6 + (P(sep),) * 5,
        out_specs=(P(leaf), P(sep)),
        check_vma=False,
    )
```

```python
import jax
import jax.numpy as jnp
from jax import lax
from jax.experimental import pallas as pl
from jax.experimental.pallas import tpu as pltpu
from jax.sharding import Mesh
from jax.sharding import PartitionSpec as P

f32 = jnp.float32
bf16 = jnp.bfloat16

B = 128
VMEM_LIMIT = 16 * 1024 * 1024


def dot(a, b):
    return jnp.dot(a, b, preferred_element_type=f32)


def dot_nt(a, b):
    return lax.dot_general(a, b, (((1,), (1,)), ((), ())), preferred_element_type=f32)


def split(x):
    high = x.astype(bf16)
    return high, (x - high.astype(f32)).astype(bf16)


def mm(a, b):
    a_high, a_low = split(a)
    b_high, b_low = split(b)
    return dot(a_high, b_high) + (dot(a_low, b_high) + dot(a_high, b_low))


def call(kernel, outs, scratch=(), name=None, smem=(), hbm=(), after=(), limit=VMEM_LIMIT):
    def run(*operands):
        count = len(operands)

        def body(*refs):
            kernel(*refs[:count], *refs[count + len(after) :])

        def space(k):
            return pltpu.SMEM if k in smem else pltpu.HBM if k in hbm else pltpu.VMEM

        return pl.pallas_call(
            body,
            out_shape=outs,
            in_specs=[pl.BlockSpec(memory_space=space(k)) for k in range(count)]
            + [pl.BlockSpec(memory_space=pl.ANY)] * len(after),
            out_specs=jax.tree.map(lambda _: pl.BlockSpec(memory_space=pltpu.VMEM), outs),
            scratch_shapes=list(scratch),
            compiler_params=pltpu.CompilerParams(vmem_limit_bytes=limit),
            name=name,
        )(*operands, *after)

    return run


def landing(arrays):
    return [pltpu.VMEM(x.shape, x.dtype) for x in arrays] + [pltpu.SemaphoreType.DMA((len(arrays),))]


def start_copies(sources, targets, sems):
    copies = [
        pltpu.make_async_copy(source, target, sems.at[k])
        for k, (source, target) in enumerate(zip(sources, targets))
    ]
    for copy in copies:
        copy.start()
    return copies


def shaped(shape, dtype):
    return jax.ShapeDtypeStruct(shape, dtype)


def scatter_updates(place_ref, got_ref, out_ref, total):
    width = out_ref.shape[-2]
    total[...] = jnp.zeros_like(total)
    for j in range(got_ref.shape[0]):
        for slot in range(8):
            s = place_ref[j, slot]
            total[s] = total[s] + got_ref[j, slot * width : (slot + 1) * width].astype(f32)
    out_ref[...] = total[...].reshape(out_ref.shape).astype(bf16)


def begin(at_ref, tgt_ref, *refs):
    sources, (mine_ref, other_ref, sent_ref), rest = refs[:8], refs[8:11], refs[11:]
    landed, sems, turned = rest[:8], rest[8], rest[9]
    copies = start_copies(sources, landed, sems)
    li_ref, ll_ref, ui_ref, ul_ref, rhs_ref, leaf_ref, inv_ref, lower_ref = landed
    groups = sent_ref.shape[0]
    width = 256 // groups
    for copy in copies[:5]:
        copy.wait()
    for s in range(2):
        turned[s] = rhs_ref[s].T
        li, ui = li_ref[s], ui_ref[s]
        blocks = (-mm(li, ll_ref[s]).T, -mm(ui, ul_ref[s]).T, li.T, ui.T)
        for ref, core in ((mine_ref, at_ref[4]), (other_ref, 1 - at_ref[4])):
            for k in range(4):
                ref[s, k * B : (k + 1) * B] = blocks[k]
            first = pl.multiple_of((2 * at_ref[0] + core) * width, width)
            ref[s, 4 * B :] = turned[s, pl.ds(first, width)]
    for copy in copies[5:]:
        copy.wait()
    for k in range(2):
        forward = dot(inv_ref[k], leaf_ref[k]).T.astype(bf16)
        for j in range(groups):
            sent_ref[j, (8 + k) * width : (9 + k) * width] = forward[j * width : (j + 1) * width]
        for i in range(4):
            update = dot_nt(forward, lower_ref[k, i]).astype(bf16)
            slot = 4 * k + i
            for j in range(groups):
                sent_ref[j, slot * width : (slot + 1) * width] = update[j * width : (j + 1) * width]
    lane = lax.broadcasted_iota(jnp.int32, (16, B), 1)
    places = jnp.zeros((16, B), jnp.int32)
    for slot in range(8):
        places = jnp.where(lane == slot, tgt_ref[slot // 4, slot % 4], places)
    for j in range(groups):
        sent_ref[j, 10 * width :] = places.astype(f32).astype(bf16)


def chip_maps(at_ref, mine_ref, other_ref, sep_ref, half_ref, wy_ref, whole):
    sep_ref[at_ref[4]] = mine_ref[...]
    sep_ref[1 - at_ref[4]] = other_ref[...]

    def block(s, k):
        return sep_ref[s // 2, s % 2, k * B : (k + 1) * B]

    reach = [block(0, 0)]
    for s in range(1, 4):
        reach.append(mm(reach[-1], block(s, 0)))
    w = mm(reach[3], block(3, 3))
    y = block(3, 1)
    wy = jnp.concatenate([w, y], axis=0)
    wy_ref[:, 3 * B :] = wy
    for s in (2, 1, 0):
        wy = mm(wy, block(s, 1))
        wy = jnp.concatenate([wy[:B] + mm(reach[s], block(s, 3)), wy[B:]], axis=0)
        wy_ref[:, s * B : (s + 1) * B] = wy
    whole[0] = reach[3]
    whole[1] = wy[B:]
    whole[2] = wy[:B]
    half_ref[...] = whole[:, pl.ds(pl.multiple_of(at_ref[4] * (B // 2), B // 2), B // 2)]


def chip_solve(got_ref, sep_ref, bg_ref, local_ref):
    total = jnp.sum(got_ref[...].astype(f32), axis=0)

    def block(s, k):
        return sep_ref[s // 2, s % 2, k * B : (k + 1) * B]

    base = [
        mm(sep_ref[s // 2, s % 2, 4 * B :] - total[s], block(s, 2)) for s in range(4)
    ]
    f = base[0]
    forward = [f]
    for s in range(1, 4):
        f = mm(f, block(s, 0)) + base[s]
        forward.append(f)
    bent = [mm(forward[s], block(s, 3)) for s in range(4)]
    u = bent[3]
    local_ref[3] = u
    for s in (2, 1, 0):
        u = mm(u, block(s, 1)) + bent[s]
        local_ref[s] = u
    for n in range(bg_ref.shape[0]):
        bg_ref[n, 0] = f.astype(bf16)
        bg_ref[n, 1] = u.astype(bf16)


def compose(maps):
    count = len(maps)
    reach = [None, maps[0][0]]
    for q in range(1, count):
        reach.append(mm(reach[-1], maps[q][0]))
    turned = [maps[0][2]] + [mm(reach[q], maps[q][2]) for q in range(1, count)]
    zy = jnp.concatenate([turned[-1], maps[-1][1]], axis=0)
    entries = [None] * count
    for q in reversed(range(count - 1)):
        entries[q] = zy
        zy = mm(zy, maps[q][1])
        zy = jnp.concatenate([zy[:B] + turned[q], zy[B:]], axis=0)
    return (reach[count], zy[B:], zy[:B]), reach[:count], entries


def keep_entries(keep, first, reach, entries):
    identity = (
        lax.broadcasted_iota(jnp.int32, (B, B), 0) == lax.broadcasted_iota(jnp.int32, (B, B), 1)
    ).astype(f32)
    for q in range(len(reach)):
        keep[first + q, 0] = identity if reach[q] is None else reach[q]
        keep[first + q, 1] = identity if entries[q] is None else entries[q][B:]
        keep[first + q, 2] = jnp.zeros((B, B), f32) if entries[q] is None else entries[q][:B]


def both(maps_ref, place, m):
    return jnp.concatenate([maps_ref[2 * place, m], maps_ref[2 * place + 1, m]], axis=0)


def col_maps(at_ref, maps_ref, quad_ref, pqr_ref, xyz_ref, keep):
    quads = []
    for h in range(4):
        maps = [[both(maps_ref, 4 * h + q, m) for m in range(3)] for q in range(4)]
        quad, reach, entries = compose(maps)
        keep_entries(keep, 4 * h, reach, entries)
        for m in range(3):
            quad_ref[h, m] = quad[m]
        quads.append(quad)
    whole, reach, entries = compose(quads)
    keep_entries(keep, 16, reach, entries)
    for m in range(3):
        pqr_ref[m] = whole[m]
    high, low = 16 + at_ref[2], 4 * at_ref[2] + at_ref[1]
    for m in range(3):
        xyz_ref[0, m] = keep[low, m]
    xyz_ref[1, 0] = mm(keep[high, 0], keep[low, 0])
    xyz_ref[1, 1] = mm(keep[high, 1], keep[low, 1])
    xyz_ref[1, 2] = mm(keep[high, 2], keep[low, 1]) + mm(keep[high, 0], keep[low, 2])


def chain(maps, bgs, keep, first):
    count = len(maps)
    f = bgs[0][0]
    entering = [None, f]
    for q in range(1, count):
        f = mm(f, maps[q][0]) + bgs[q][0]
        entering.append(f)
    turned = [bgs[0][1]] + [mm(entering[q], maps[q][2]) + bgs[q][1] for q in range(1, count)]
    keep[first, 0] = jnp.zeros_like(f)
    keep[first + count - 1, 1] = jnp.zeros_like(f)
    for q in range(1, count):
        keep[first + q, 0] = entering[q]
    u = turned[-1]
    for q in reversed(range(count - 1)):
        keep[first + q, 1] = u
        u = mm(u, maps[q][1]) + turned[q]
    return f, u


def col_solve(at_ref, maps_ref, quad_ref, bg_ref, xyz_ref, pqr_ref, out_ref, own_ref, keep):
    width = bg_ref.shape[2]
    quads = []
    for h in range(4):
        places = range(4 * h, 4 * h + 4)
        maps = [[both(maps_ref, p, m) for m in range(3)] for p in places]
        bgs = [[bg_ref[p, m].astype(f32) for m in range(2)] for p in places]
        quads.append(chain(maps, bgs, keep, 4 * h))
    maps = [[quad_ref[h, m] for m in range(3)] for h in range(4)]
    f, u = chain(maps, quads, keep, 16)
    for n in range(out_ref.shape[0]):
        for m in range(3):
            out_ref[n, m * B : (m + 1) * B] = pqr_ref[m]
        out_ref[n, 3 * B : 3 * B + width] = f
        out_ref[n, 3 * B + width :] = u
    high, low = 16 + at_ref[2], 4 * at_ref[2] + at_ref[1]
    f, u = keep[high, 0], keep[high, 1]
    own_ref[0] = mm(f, xyz_ref[0, 0]) + keep[low, 0]
    own_ref[1] = mm(u, xyz_ref[0, 1]) + mm(f, xyz_ref[0, 2]) + keep[low, 1]


def top_solve(at_ref, got_ref, xyz_ref, own_ref, wy_ref, local_ref, sep_ref, low_ref, keep):
    width = own_ref.shape[1]
    count = got_ref.shape[0]
    maps = [[got_ref[q, m * B : (m + 1) * B] for m in range(3)] for q in range(count)]
    bgs = [
        [got_ref[q, 3 * B + m * width : 3 * B + (m + 1) * width] for m in range(2)] for q in range(count)
    ]
    chain(maps, bgs, keep, 0)
    f, u = keep[at_ref[3], 0], keep[at_ref[3], 1]
    f, u = (
        mm(f, xyz_ref[1, 0]) + own_ref[0],
        mm(u, xyz_ref[1, 1]) + mm(f, xyz_ref[1, 2]) + own_ref[1],
    )
    reached = mm(jnp.concatenate([f, u], axis=1), wy_ref[...])
    for s in range(4):
        value = local_ref[s] + reached[:, s * B : (s + 1) * B]
        high, rest = split(value)
        sep_ref[s // 2, s % 2, 0] = high
        sep_ref[s // 2, s % 2, 1] = rest
        for n in range(low_ref.shape[0]):
            low_ref[n, s] = high


def leaf_backward(place_ref, solved_ref, got_ref, upper_ref, sep_ref, out_ref):
    width = out_ref.shape[2]
    for j in range(out_ref.shape[0]):
        for k in range(2):
            total = jnp.zeros((width, B), f32)
            for i in range(4):
                total = total + dot_nt(solved_ref[place_ref[j, 4 * k + i]], upper_ref[j, k, i])
            forward = got_ref[j, (8 + k) * width : (9 + k) * width].astype(f32)
            out_ref[j, k] = dot_nt((forward - total).astype(bf16), upper_ref[j, k, 4]).astype(bf16)
            out_ref[j, 2 + 2 * k] = sep_ref[j % 2, k, 0]
            out_ref[j, 3 + 2 * k] = sep_ref[j % 2, k, 1]


def turn_back(got_ref, leaf_ref, sep_ref):
    width = got_ref.shape[2]
    for j in range(got_ref.shape[0]):
        lanes = pl.ds(j * width, width)
        for k in range(2):
            leaf_ref[k, :, lanes] = got_ref[j, k].astype(f32).T.astype(bf16)
            value = got_ref[j, 2 + 2 * k].astype(f32) + got_ref[j, 3 + 2 * k].astype(f32)
            sep_ref[k, :, lanes] = value.T


def exchange(value, axes):
    return lax.all_to_all(value, axes, split_axis=0, concat_axis=0, tiled=True)


def on_device(
    leaf_rhs,
    leaf_lower_inv,
    leaf_upper_inv,
    leaf_lower,
    leaf_upper,
    targets,
    sep_rhs,
    sep_lower_inv,
    sep_upper_inv,
    sep_lower_link,
    sep_upper_link,
):
    across = ("layer", "core")
    layers, rows = lax.axis_size("layer"), lax.axis_size("row")
    highs, lows = lax.axis_size("zh"), lax.axis_size("zl")
    groups = 2 * layers
    width = 256 // groups
    chips = highs * lows
    at = jnp.stack(
        [lax.axis_index(name) for name in ("layer", "zl", "zh", "row", "core")]
    ).astype(jnp.int32)

    along = ("zh", "zl")
    pair = (2, width, B)

    sources = (
        sep_lower_inv,
        sep_lower_link,
        sep_upper_inv,
        sep_upper_link,
        sep_rhs,
        leaf_rhs,
        leaf_lower_inv,
        leaf_lower,
    )
    blocks = shaped((2, 4 * B + width, B), f32)
    mine, others, sent = call(
        begin,
        (blocks, blocks, shaped((groups, 10 * width + 16, B), bf16)),
        landing(sources) + [pltpu.VMEM((2, 256, B), f32)],
        "begin",
        smem=(0, 1),
        hbm=range(2, 10),
        limit=60 * 1024 * 1024,
    )(at, targets, *sources)
    theirs = lax.ppermute(others, "core", [(0, 1), (1, 0)])
    got = exchange(sent, across)
    place = got[:, 10 * width, :8].astype(jnp.int32)
    seps, half, wy = call(
        chip_maps,
        (shaped((2, 2, 4 * B + width, B), f32), shaped((3, B // 2, B), f32), shaped((2 * B, 4 * B), f32)),
        [pltpu.VMEM((3, B, B), f32)],
        "chip_maps",
        smem=(0,),
    )(at, mine, theirs)
    maps = lax.all_gather(half, along + ("core",))
    upper = lax.all_gather(jnp.concatenate([leaf_upper, leaf_upper_inv[:, None]], axis=1), across)

    sums = call(
        scatter_updates,
        shaped((chips, 4, width, B), bf16),
        [pltpu.VMEM((4 * chips, width, B), f32)],
        "scatter_updates",
        (0,),
        after=(half,),
    )(place, got)
    bg, local = call(
        chip_solve,
        (shaped((chips,) + pair, bf16), shaped((4, width, B), f32)),
        name="chip_solve",
    )(exchange(sums, along), seps)
    quads, pqr, xyz = call(
        col_maps,
        (shaped((4, 3, B, B), f32), shaped((3, B, B), f32), shaped((2, 3, B, B), f32)),
        [pltpu.VMEM((20, 3, B, B), f32)],
        "col_maps",
        (0,),
    )(at, maps)
    sent_on, own = call(
        col_solve,
        (shaped((rows, 3 * B + 2 * width, B), f32), shaped(pair, f32)),
        [pltpu.VMEM((20,) + pair, f32)],
        "col_solve",
        (0,),
    )(at, maps, quads, exchange(bg, along), xyz, pqr)
    solved, solved_low = call(
        top_solve,
        (shaped((2, 2, 2, width, B), bf16), shaped((chips, 4, width, B), bf16)),
        [pltpu.VMEM((rows,) + pair, f32)],
        "top_solve",
        (0,),
    )(at, exchange(sent_on, "row"), xyz, own, wy, local)

    low = exchange(solved_low, along).reshape(4 * chips, width, B)
    back = call(
        leaf_backward, shaped((groups, 6, width, B), bf16), name="leaf_backward", smem=(0,)
    )(place, low, got, upper, solved)
    return call(turn_back, (shaped((2, B, 256), bf16), shaped((2, B, 256), f32)), name="turn_back")(
        exchange(back, across)
    )


def solution(mesh):
    layers, rows, cols = (mesh.shape[name] for name in ("layer", "row", "col"))
    lows = 4
    fine = Mesh(
        mesh.devices.reshape(layers, rows, cols // (2 * lows), lows, 2),
        ("layer", "row", "zh", "zl", "core"),
    )
    leaf = ("layer", "row", "zh", "zl", "core")
    sep = ("row", "zh", "zl", "core")
    return jax.shard_map(
        on_device,
        mesh=fine,
        in_specs=(P(leaf),) * 6 + (P(sep),) * 5,
        out_specs=(P(leaf), P(sep)),
        check_vma=False,
    )
```

```python
import jax
import jax.numpy as jnp
from jax import lax
from jax.experimental import pallas as pl
from jax.experimental.pallas import tpu as pltpu
from jax.sharding import Mesh
from jax.sharding import PartitionSpec as P

f32 = jnp.float32
bf16 = jnp.bfloat16

B = 128
VMEM_LIMIT = 16 * 1024 * 1024
VMEM_ALL = 60 * 1024 * 1024


def dot(a, b):
    return jnp.dot(a, b, preferred_element_type=f32)


def dot_nt(a, b):
    return lax.dot_general(a, b, (((1,), (1,)), ((), ())), preferred_element_type=f32)


def split(x):
    high = x.astype(bf16)
    return high, (x - high.astype(f32)).astype(bf16)


def mm(a, b):
    a_high, a_low = split(a)
    b_high, b_low = split(b)
    if b.shape == (B, B):
        wide = jnp.concatenate([b_high, b_low], axis=1)
        parts = dot(jnp.concatenate([a_high, a_low], axis=1), jnp.concatenate([wide, wide], axis=0))
        return parts[:, :B] + parts[:, B:]
    return dot(a_high, b_high) + (dot(a_low, b_high) + dot(a_high, b_low))


def call(kernel, outs, scratch=(), name=None, smem=(), hbm=(), after=(), limit=VMEM_LIMIT):
    def run(*operands):
        count = len(operands)

        def body(*refs):
            kernel(*refs[:count], *refs[count + len(after) :])

        def space(k):
            return pltpu.SMEM if k in smem else pltpu.HBM if k in hbm else pltpu.VMEM

        return pl.pallas_call(
            body,
            out_shape=outs,
            in_specs=[pl.BlockSpec(memory_space=space(k)) for k in range(count)]
            + [pl.BlockSpec(memory_space=pl.ANY)] * len(after),
            out_specs=jax.tree.map(lambda _: pl.BlockSpec(memory_space=pltpu.VMEM), outs),
            scratch_shapes=list(scratch),
            compiler_params=pltpu.CompilerParams(vmem_limit_bytes=limit),
            name=name,
        )(*operands, *after)

    return run


def landing(arrays):
    return [pltpu.VMEM(x.shape, x.dtype) for x in arrays] + [pltpu.SemaphoreType.DMA((len(arrays),))]


def start_copies(sources, targets, sems):
    copies = [
        pltpu.make_async_copy(source, target, sems.at[k])
        for k, (source, target) in enumerate(zip(sources, targets))
    ]
    for copy in copies:
        copy.start()
    return copies


def shaped(shape, dtype):
    return jax.ShapeDtypeStruct(shape, dtype)


def scatter_updates(place_ref, got_ref, out_ref, forward_ref, total):
    width = out_ref.shape[-2]
    total[...] = jnp.zeros_like(total)
    for j in range(got_ref.shape[0]):
        for slot in range(8):
            s = place_ref[j, slot]
            total[s] = total[s] + got_ref[j, slot * width : (slot + 1) * width].astype(f32)
    out_ref[...] = total[...].reshape(out_ref.shape).astype(bf16)
    for k in range(2):
        forward_ref[:, k] = got_ref[:, (8 + k) * width : (9 + k) * width]


def leaf_forward(tgt_ref, *refs):
    sources, sent_ref, landed, sems = refs[:3], refs[3], refs[4:7], refs[7]
    copies = start_copies(sources, landed, sems)
    rhs_ref, inv_ref, lower_ref = landed
    groups = sent_ref.shape[0]
    width = 256 // groups
    lane = lax.broadcasted_iota(jnp.int32, (16, B), 1)
    places = jnp.zeros((16, B), jnp.int32)
    for slot in range(8):
        places = jnp.where(lane == slot, tgt_ref[slot // 4, slot % 4], places)
    for j in range(groups):
        sent_ref[j, 10 * width :] = places.astype(f32).astype(bf16)
    copies[0].wait()
    copies[1].wait()
    forwards = []
    for k in range(2):
        forward = dot(inv_ref[k], rhs_ref[k]).T.astype(bf16)
        forwards.append(forward)
        for j in range(groups):
            sent_ref[j, (8 + k) * width : (9 + k) * width] = forward[j * width : (j + 1) * width]
    copies[2].wait()
    for k in range(2):
        for i in range(4):
            update = dot_nt(forwards[k], lower_ref[k, i]).astype(bf16)
            slot = 4 * k + i
            for j in range(groups):
                sent_ref[j, slot * width : (slot + 1) * width] = update[j * width : (j + 1) * width]


def sep_prepare(at_ref, *refs):
    sources, (mine_ref, other_ref), landed, sems, turned = refs[:5], refs[5:7], refs[7:12], refs[12], refs[13]
    copies = start_copies(sources, landed, sems)
    li_ref, ll_ref, ui_ref, ul_ref, rhs_ref = landed
    width = mine_ref.shape[1] - 4 * B
    for copy in copies:
        copy.wait()
    for s in range(2):
        turned[s] = rhs_ref[s].T
        li, ui = li_ref[s], ui_ref[s]
        blocks = (-mm(li, ll_ref[s]).T, -mm(ui, ul_ref[s]).T, li.T, ui.T)
        for ref, core in ((mine_ref, at_ref[4]), (other_ref, 1 - at_ref[4])):
            for k in range(4):
                ref[s, k * B : (k + 1) * B] = blocks[k]
            first = pl.multiple_of((2 * at_ref[0] + core) * width, width)
            ref[s, 4 * B :] = turned[s, pl.ds(first, width)]


def map_parts(maps):
    return split(maps[0]) + split(maps[1]) + (maps[2].astype(bf16),)


def send_half(at_ref, maps, half_ref, whole):
    for m, part in enumerate(map_parts(maps)):
        whole[m] = part
    half_ref[...] = whole[:, pl.ds(pl.multiple_of(at_ref[4] * (B // 2), B // 2), B // 2)]


def chip_maps(at_ref, mine_ref, other_ref, sep_ref, half_ref, wy_ref, whole):
    sep_ref[at_ref[4]] = mine_ref[...]
    sep_ref[1 - at_ref[4]] = other_ref[...]

    def block(s, k):
        return sep_ref[s // 2, s % 2, k * B : (k + 1) * B]

    reach = [block(0, 0)]
    for s in range(1, 4):
        reach.append(mm(reach[-1], block(s, 0)))
    w = mm(reach[3], block(3, 3))
    y = block(3, 1)
    wy = jnp.concatenate([w, y], axis=0)
    wy_ref[:, 3 * B :] = wy
    for s in (2, 1, 0):
        wy = mm(wy, block(s, 1))
        wy = jnp.concatenate([wy[:B] + mm(reach[s], block(s, 3)), wy[B:]], axis=0)
        wy_ref[:, s * B : (s + 1) * B] = wy
    send_half(at_ref, (reach[3], wy[B:], wy[:B]), half_ref, whole)


def chip_solve(got_ref, sep_ref, bg_ref, local_ref):
    total = jnp.sum(got_ref[...].astype(f32), axis=0)

    def block(s, k):
        return sep_ref[s // 2, s % 2, k * B : (k + 1) * B]

    base = [
        mm(sep_ref[s // 2, s % 2, 4 * B :] - total[s], block(s, 2)) for s in range(4)
    ]
    f = base[0]
    forward = [f]
    for s in range(1, 4):
        f = mm(f, block(s, 0)) + base[s]
        forward.append(f)
    bent = [mm(forward[s], block(s, 3)) for s in range(4)]
    u = bent[3]
    local_ref[3] = u
    for s in (2, 1, 0):
        u = mm(u, block(s, 1)) + bent[s]
        local_ref[s] = u
    for n in range(bg_ref.shape[0]):
        bg_ref[n, 0] = f.astype(bf16)
        bg_ref[n, 1] = u.astype(bf16)


def mm_parts(a, high, low):
    a_high, a_low = split(a)
    wide = jnp.concatenate([high, low], axis=1)
    parts = dot(jnp.concatenate([a_high, a_low], axis=1), jnp.concatenate([wide, wide], axis=0))
    return parts[:, :B] + parts[:, B:]


def mm_two(a, b_high, b_low, c_high, c_low):
    a_high, a_low = split(a)
    high = jnp.concatenate([b_high, c_high], axis=1)
    both = dot(jnp.concatenate([a_high, a_low], axis=1), jnp.concatenate([high, high], axis=0))
    if c_low is None:
        return both[:, :B] + dot(a_high, b_low), both[:, B:]
    both = both + dot(a_high, jnp.concatenate([b_low, c_low], axis=1))
    return both[:, :B], both[:, B:]


def compose(maps, sides):
    count = len(maps)
    whole = [sum(part.astype(f32) for part in m if part is not None) for m in maps[0]]
    none = jnp.zeros((B, B), f32)
    rows = jnp.concatenate([whole[0], sides[0][0]], axis=0)
    bent = [jnp.concatenate([whole[2], sides[0][1]], axis=0)]
    entering = [None, rows]
    for q in range(1, count):
        rows, turned = mm_two(rows, *maps[q][0], *maps[q][2])
        rows = rows + jnp.concatenate([none, sides[q][0]], axis=0)
        bent.append(turned + jnp.concatenate([none, sides[q][1]], axis=0))
        entering.append(rows)
    last = sum(part.astype(f32) for part in maps[-1][1])
    back = jnp.concatenate([bent[-1], last], axis=0)
    leaving = [None] * count
    for q in reversed(range(count - 1)):
        leaving[q] = back
        back = mm_parts(back, *maps[q][1])
        size = bent[q].shape[0]
        back = jnp.concatenate([back[:size] + bent[q], back[size:]], axis=0)
    size = bent[0].shape[0]
    whole = (rows[:B], back[size:], back[:B])
    return whole, (rows[B:], back[B:size]), entering[:count], leaving


def keep_entries(keep_maps, keep, first, entering, leaving, width):
    identity = (
        lax.broadcasted_iota(jnp.int32, (B, B), 0) == lax.broadcasted_iota(jnp.int32, (B, B), 1)
    ).astype(f32)
    none, nothing = jnp.zeros((B, B), f32), jnp.zeros((width, B), f32)
    for q in range(len(entering)):
        f, u = entering[q], leaving[q]
        keep_maps[first + q, 0] = identity if f is None else f[:B]
        keep[first + q, 0] = nothing if f is None else f[B:]
        keep_maps[first + q, 1] = identity if u is None else u[B + width :]
        keep_maps[first + q, 2] = none if u is None else u[:B]
        keep[first + q, 1] = nothing if u is None else u[B : B + width]


def row_solve(at_ref, maps_hbm, bg_ref, out_ref, xyz_ref, own_ref, maps_ref, sems, keep_maps, keep):
    width = bg_ref.shape[2]
    quads = [pl.ds(8 * h, 8) for h in range(4)]
    copies = start_copies([maps_hbm.at[q] for q in quads], [maps_ref.at[q] for q in quads], sems)
    quad_maps, quad_sides = [], []
    for h in range(4):
        copies[h].wait()
        maps, sides = [], []
        for p in range(4 * h, 4 * h + 4):
            part = [
                jnp.concatenate([maps_ref[2 * p, m], maps_ref[2 * p + 1, m]], axis=0) for m in range(5)
            ]
            maps.append((part[:2], part[2:4], (part[4], None)))
            sides.append([bg_ref[p, m].astype(f32) for m in range(2)])
        quad, side, entering, leaving = compose(maps, sides)
        keep_entries(keep_maps, keep, 4 * h, entering, leaving, width)
        quad_maps.append([split(m) for m in quad])
        quad_sides.append(side)
    row, side, entering, leaving = compose(quad_maps, quad_sides)
    keep_entries(keep_maps, keep, 16, entering, leaving, width)
    sent = map_parts(row)
    sides = split(side[0]) + split(side[1])
    for n in range(out_ref.shape[0]):
        for m in range(5):
            out_ref[n, m * B : (m + 1) * B] = sent[m]
        for m in range(4):
            out_ref[n, 5 * B + m * width : 5 * B + (m + 1) * width] = sides[m]
    high, low = 16 + at_ref[2], 4 * at_ref[2] + at_ref[1]
    x, y, z = (keep_maps[low, m] for m in range(3))
    f = mm(jnp.concatenate([keep_maps[high, 0], keep[high, 0]], axis=0), x)
    u = mm(jnp.concatenate([keep_maps[high, 2], keep_maps[high, 1], keep[high, 1]], axis=0), y)
    z = mm(jnp.concatenate([keep_maps[high, 0], keep[high, 0]], axis=0), z)
    xyz_ref[0] = f[:B]
    xyz_ref[1] = u[B : 2 * B]
    xyz_ref[2] = u[:B] + z[:B]
    own_ref[0] = f[B:] + keep[low, 0]
    own_ref[1] = u[2 * B :] + z[B:] + keep[low, 1]


def chain(maps, bgs, keep):
    count = len(maps)
    f = bgs[0][0]
    entering = [None, f]
    for q in range(1, count - 1):
        f = mm(f, maps[q][0]) + bgs[q][0]
        entering.append(f)
    turned = [None] + [mm(entering[q], maps[q][2]) + bgs[q][1] for q in range(1, count)]
    keep[0, 0] = jnp.zeros_like(f)
    keep[count - 1, 1] = jnp.zeros_like(f)
    for q in range(1, count):
        keep[q, 0] = entering[q]
    u = turned[-1]
    for q in reversed(range(count - 1)):
        keep[q, 1] = u
        if q > 0:
            u = mm(u, maps[q][1]) + turned[q]


def top_solve(at_ref, got_ref, xyz_ref, own_ref, wy_ref, local_ref, sep_ref, low_ref, keep):
    width = own_ref.shape[1]
    count = got_ref.shape[0]
    maps, bgs = [], []
    for q in range(count):
        part = [got_ref[q, m * B : (m + 1) * B].astype(f32) for m in range(5)]
        maps.append([part[0] + part[1], part[2] + part[3], part[4]])
        side = [
            got_ref[q, 5 * B + m * width : 5 * B + (m + 1) * width].astype(f32) for m in range(4)
        ]
        bgs.append([side[0] + side[1], side[2] + side[3]])
    chain(maps, bgs, keep)
    f, u = keep[at_ref[3], 0], keep[at_ref[3], 1]
    f, u = (
        mm(f, xyz_ref[0]) + own_ref[0],
        mm(u, xyz_ref[1]) + mm(f, xyz_ref[2]) + own_ref[1],
    )
    reached = mm(jnp.concatenate([f, u], axis=1), wy_ref[...])
    for s in range(4):
        value = local_ref[s] + reached[:, s * B : (s + 1) * B]
        sep_ref[s] = value
        low = value.astype(bf16)
        for n in range(low_ref.shape[0]):
            low_ref[n, s] = low


def join_upper(upper_ref, inv_ref, out_ref):
    for k in range(2):
        for i in range(4):
            out_ref[k, i * B : (i + 1) * B] = upper_ref[k, i].astype(f32).T.astype(bf16)
        out_ref[k, 4 * B :] = inv_ref[k].astype(f32).T.astype(bf16)


def leaf_backward(place_ref, solved_ref, forward_ref, upper_ref, out_ref):
    for j in range(out_ref.shape[0]):
        for k in range(2):
            solved = [solved_ref[place_ref[j, 4 * k + i]] for i in range(4)]
            total = dot(jnp.concatenate(solved, axis=1), upper_ref[j, k, : 4 * B])
            residual = (forward_ref[j, k].astype(f32) - total).astype(bf16)
            out_ref[j, k] = dot(residual, upper_ref[j, k, 4 * B :]).astype(bf16)


def turn_leaf(got_ref, out_ref):
    width = got_ref.shape[2]
    for k in range(2):
        whole = jnp.concatenate([got_ref[j, k] for j in range(got_ref.shape[0])], axis=0)
        out_ref[k] = whole.astype(f32).T.astype(bf16)


def turn_sep(at_ref, got_ref, out_ref):
    for k in range(2):
        s = 2 * at_ref[4] + k
        whole = jnp.concatenate([got_ref[j, s] for j in range(got_ref.shape[0])], axis=0)
        out_ref[k] = whole.T


def exchange(value, axes):
    return lax.all_to_all(value, axes, split_axis=0, concat_axis=0, tiled=True)


def on_device(
    leaf_rhs,
    leaf_lower_inv,
    leaf_upper_inv,
    leaf_lower,
    leaf_upper,
    targets,
    sep_rhs,
    sep_lower_inv,
    sep_upper_inv,
    sep_lower_link,
    sep_upper_link,
):
    across = ("layer", "core")
    layers, rows = lax.axis_size("layer"), lax.axis_size("row")
    highs, lows = lax.axis_size("zh"), lax.axis_size("zl")
    groups = 2 * layers
    width = 256 // groups
    chips = highs * lows
    at = jnp.stack(
        [lax.axis_index(name) for name in ("layer", "zl", "zh", "row", "core")]
    ).astype(jnp.int32)

    along = ("zh", "zl")
    pair = (2, width, B)

    sources = (sep_lower_inv, sep_lower_link, sep_upper_inv, sep_upper_link, sep_rhs)
    blocks = shaped((2, 4 * B + width, B), f32)
    half_maps = shaped((5, B // 2, B), bf16)
    maps = shaped((3, B, B), f32)
    mine, others = call(
        sep_prepare,
        (blocks, blocks),
        landing(sources) + [pltpu.VMEM((2, 256, B), f32)],
        "sep_prepare",
        smem=(0,),
        hbm=range(1, 6),
        limit=VMEM_ALL,
    )(at, *sources)
    theirs = lax.ppermute(others, "core", [(0, 1), (1, 0)])

    sources = (leaf_rhs, leaf_lower_inv, leaf_lower)
    sent = call(
        leaf_forward,
        shaped((groups, 10 * width + 16, B), bf16),
        landing(sources),
        "leaf_forward",
        smem=(0,),
        hbm=(1, 2, 3),
        limit=VMEM_ALL,
        after=(mine,),
    )(targets, *sources)
    seps, half, wy = call(
        chip_maps,
        (shaped((2, 2, 4 * B + width, B), f32), half_maps, shaped((2 * B, 4 * B), f32)),
        [pltpu.VMEM((5, B, B), bf16)],
        "chip_maps",
        smem=(0,),
        limit=VMEM_ALL,
        after=(sent,),
    )(at, mine, theirs)
    by_chip = lax.all_gather(half, along + ("core",)).reshape((2 * chips,) + half_maps.shape)

    got = exchange(sent, across)
    place = got[:, 10 * width, :8].astype(jnp.int32)
    sums, forward = call(
        scatter_updates,
        (shaped((chips, 4, width, B), bf16), shaped((groups, 2, width, B), bf16)),
        [pltpu.VMEM((4 * chips, width, B), f32)],
        "scatter_updates",
        smem=(0,),
        after=(half,),
    )(place, got)

    bg, local = call(
        chip_solve, (shaped((chips,) + pair, bf16), shaped((4, width, B), f32)), name="chip_solve"
    )(exchange(sums, along), seps)
    sent_on, xyz, own = call(
        row_solve,
        (shaped((rows, 5 * B + 4 * width, B), bf16), maps, shaped(pair, f32)),
        [
            pltpu.VMEM((2 * chips,) + half_maps.shape, bf16),
            pltpu.SemaphoreType.DMA((4,)),
            pltpu.VMEM((20, 3, B, B), f32),
            pltpu.VMEM((20,) + pair, f32),
        ],
        "row_solve",
        smem=(0,),
        hbm=(1,),
        limit=VMEM_ALL,
    )(at, by_chip, exchange(bg, along))
    solved, solved_low = call(
        top_solve,
        (shaped((4, width, B), f32), shaped((chips, 4, width, B), bf16)),
        [pltpu.VMEM((rows,) + pair, f32)],
        "top_solve",
        smem=(0,),
        limit=VMEM_ALL,
    )(at, exchange(sent_on, "row"), xyz, own, wy, local)

    joined = call(
        join_upper, shaped((2, 5 * B, B), bf16), name="join_upper", after=(sums,), limit=VMEM_ALL
    )(leaf_upper, leaf_upper_inv)
    upper = lax.all_gather(joined, across).reshape((groups, 2, 5 * B, B))
    low = exchange(solved_low, along).reshape(4 * chips, width, B)
    sep_all = lax.all_gather(solved, across).reshape((groups, 4, width, B))
    sep_part = call(turn_sep, shaped((2, B, 256), f32), name="turn_sep", smem=(0,))(at, sep_all)
    back = call(
        leaf_backward,
        shaped((groups, 2, width, B), bf16),
        name="leaf_backward",
        smem=(0,),
        after=(sep_part,),
    )(place, low, forward, upper)
    leaf_part = call(turn_leaf, shaped((2, B, 256), bf16), name="turn_leaf")(exchange(back, across))
    return (leaf_part, sep_part)


def solution(mesh):
    layers, rows, cols = (mesh.shape[name] for name in ("layer", "row", "col"))
    lows = 4
    fine = Mesh(
        mesh.devices.reshape(layers, rows, cols // (2 * lows), lows, 2),
        ("layer", "row", "zh", "zl", "core"),
    )
    leaf = ("layer", "row", "zh", "zl", "core")
    sep = ("row", "zh", "zl", "core")
    return jax.shard_map(
        on_device,
        mesh=fine,
        in_specs=(P(leaf),) * 6 + (P(sep),) * 5,
        out_specs=(P(leaf), P(sep)),
        check_vma=False,
    )
```

```python
import jax
import jax.numpy as jnp
from jax import lax
from jax.experimental import pallas as pl
from jax.experimental.pallas import tpu as pltpu
from jax.sharding import Mesh
from jax.sharding import PartitionSpec as P

f32 = jnp.float32
bf16 = jnp.bfloat16

B = 128
VMEM_LIMIT = 16 * 1024 * 1024
VMEM_ALL = 60 * 1024 * 1024


def dot(a, b):
    return jnp.dot(a, b, preferred_element_type=f32)


def dot_nt(a, b):
    return lax.dot_general(a, b, (((1,), (1,)), ((), ())), preferred_element_type=f32)


def split(x):
    high = x.astype(bf16)
    return high, (x - high.astype(f32)).astype(bf16)


def mm(a, b):
    a_high, a_low = split(a)
    b_high, b_low = split(b)
    if b.shape == (B, B):
        wide = jnp.concatenate([b_high, b_low], axis=1)
        parts = dot(jnp.concatenate([a_high, a_low], axis=1), jnp.concatenate([wide, wide], axis=0))
        return parts[:, :B] + parts[:, B:]
    return dot(a_high, b_high) + (dot(a_low, b_high) + dot(a_high, b_low))


def call(kernel, outs, scratch=(), name=None, smem=(), hbm=(), after=(), limit=VMEM_LIMIT):
    def run(*operands):
        count = len(operands)

        def body(*refs):
            kernel(*refs[:count], *refs[count + len(after) :])

        def space(k):
            return pltpu.SMEM if k in smem else pltpu.HBM if k in hbm else pltpu.VMEM

        return pl.pallas_call(
            body,
            out_shape=outs,
            in_specs=[pl.BlockSpec(memory_space=space(k)) for k in range(count)]
            + [pl.BlockSpec(memory_space=pl.ANY)] * len(after),
            out_specs=jax.tree.map(lambda _: pl.BlockSpec(memory_space=pltpu.VMEM), outs),
            scratch_shapes=list(scratch),
            compiler_params=pltpu.CompilerParams(vmem_limit_bytes=limit),
            name=name,
        )(*operands, *after)

    return run


def landing(arrays):
    return [pltpu.VMEM(x.shape, x.dtype) for x in arrays] + [pltpu.SemaphoreType.DMA((len(arrays),))]


def start_copies(sources, targets, sems):
    copies = [
        pltpu.make_async_copy(source, target, sems.at[k])
        for k, (source, target) in enumerate(zip(sources, targets))
    ]
    for copy in copies:
        copy.start()
    return copies


def shaped(shape, dtype):
    return jax.ShapeDtypeStruct(shape, dtype)


def scatter_updates(place_ref, got_ref, out_ref, forward_ref, total):
    width = out_ref.shape[-2]
    total[...] = jnp.zeros_like(total)
    for j in range(got_ref.shape[0]):
        for slot in range(8):
            s = place_ref[j, slot]
            total[s] = total[s] + got_ref[j, slot * width : (slot + 1) * width].astype(f32)
    out_ref[...] = total[...].reshape(out_ref.shape).astype(bf16)
    for k in range(2):
        forward_ref[:, k] = got_ref[:, (8 + k) * width : (9 + k) * width]


def leaf_forward(tgt_ref, *refs):
    sources, sent_ref, landed, sems = refs[:3], refs[3], refs[4:7], refs[7]
    copies = start_copies(sources, landed, sems)
    rhs_ref, inv_ref, lower_ref = landed
    groups = sent_ref.shape[0]
    width = 256 // groups
    lane = lax.broadcasted_iota(jnp.int32, (16, B), 1)
    places = jnp.zeros((16, B), jnp.int32)
    for slot in range(8):
        places = jnp.where(lane == slot, tgt_ref[slot // 4, slot % 4], places)
    for j in range(groups):
        sent_ref[j, 10 * width :] = places.astype(f32).astype(bf16)
    copies[0].wait()
    copies[1].wait()
    forwards = []
    for k in range(2):
        forward = dot(inv_ref[k], rhs_ref[k]).T.astype(bf16)
        forwards.append(forward)
        for j in range(groups):
            sent_ref[j, (8 + k) * width : (9 + k) * width] = forward[j * width : (j + 1) * width]
    copies[2].wait()
    for k in range(2):
        for i in range(4):
            update = dot_nt(forwards[k], lower_ref[k, i]).astype(bf16)
            slot = 4 * k + i
            for j in range(groups):
                sent_ref[j, slot * width : (slot + 1) * width] = update[j * width : (j + 1) * width]


def sep_prepare(*refs):
    sources, (mine_ref, other_ref), landed, sems, turned = refs[:5], refs[5:7], refs[7:12], refs[12], refs[13]
    copies = start_copies(sources, landed, sems)
    li_ref, ll_ref, ui_ref, ul_ref, rhs_ref = landed
    width = mine_ref.shape[1] - 4 * B
    for copy in copies:
        copy.wait()
    for s in range(2):
        turned[s] = rhs_ref[s].T
        li, ui = li_ref[s], ui_ref[s]
        blocks = (-mm(li, ll_ref[s]).T, -mm(ui, ul_ref[s]).T, li.T, ui.T)
        for ref, core in ((mine_ref, lax.axis_index("core")), (other_ref, 1 - lax.axis_index("core"))):
            for k in range(4):
                ref[s, k * B : (k + 1) * B] = blocks[k]
            first = pl.multiple_of((2 * lax.axis_index("layer") + core) * width, width)
            ref[s, 4 * B :] = turned[s, pl.ds(first, width)]


def map_parts(maps):
    return split(maps[0]) + split(maps[1]) + (maps[2].astype(bf16),)


def send_half(maps, half_ref, whole):
    for m, part in enumerate(map_parts(maps)):
        whole[m] = part
    half_ref[...] = whole[:, pl.ds(pl.multiple_of(lax.axis_index("core") * (B // 2), B // 2), B // 2)]


def chip_maps(mine_ref, other_ref, sep_ref, half_ref, wy_ref, whole):
    sep_ref[lax.axis_index("core")] = mine_ref[...]
    sep_ref[1 - lax.axis_index("core")] = other_ref[...]

    def block(s, k):
        return sep_ref[s // 2, s % 2, k * B : (k + 1) * B]

    reach = [block(0, 0)]
    for s in range(1, 4):
        reach.append(mm(reach[-1], block(s, 0)))
    w = mm(reach[3], block(3, 3))
    y = block(3, 1)
    wy = jnp.concatenate([w, y], axis=0)
    wy_ref[:, 3 * B :] = wy
    for s in (2, 1, 0):
        wy = mm(wy, block(s, 1))
        wy = jnp.concatenate([wy[:B] + mm(reach[s], block(s, 3)), wy[B:]], axis=0)
        wy_ref[:, s * B : (s + 1) * B] = wy
    send_half((reach[3], wy[B:], wy[:B]), half_ref, whole)


def chip_solve(got_ref, sep_ref, bg_ref, local_ref):
    total = jnp.sum(got_ref[...].astype(f32), axis=0)

    def block(s, k):
        return sep_ref[s // 2, s % 2, k * B : (k + 1) * B]

    base = [
        mm(sep_ref[s // 2, s % 2, 4 * B :] - total[s], block(s, 2)) for s in range(4)
    ]
    f = base[0]
    forward = [f]
    for s in range(1, 4):
        f = mm(f, block(s, 0)) + base[s]
        forward.append(f)
    bent = [mm(forward[s], block(s, 3)) for s in range(4)]
    u = bent[3]
    local_ref[3] = u
    for s in (2, 1, 0):
        u = mm(u, block(s, 1)) + bent[s]
        local_ref[s] = u
    for n in range(bg_ref.shape[0]):
        bg_ref[n, 0] = f.astype(bf16)
        bg_ref[n, 1] = u.astype(bf16)


def mm_parts(a, high, low):
    a_high, a_low = split(a)
    wide = jnp.concatenate([high, low], axis=1)
    parts = dot(jnp.concatenate([a_high, a_low], axis=1), jnp.concatenate([wide, wide], axis=0))
    return parts[:, :B] + parts[:, B:]


def mm_two(a, b_high, b_low, c_high, c_low):
    a_high, a_low = split(a)
    high = jnp.concatenate([b_high, c_high], axis=1)
    both = dot(jnp.concatenate([a_high, a_low], axis=1), jnp.concatenate([high, high], axis=0))
    if c_low is None:
        return both[:, :B] + dot(a_high, b_low), both[:, B:]
    both = both + dot(a_high, jnp.concatenate([b_low, c_low], axis=1))
    return both[:, :B], both[:, B:]


def compose(maps, sides):
    count = len(maps)
    whole = [sum(part.astype(f32) for part in m if part is not None) for m in maps[0]]
    none = jnp.zeros((B, B), f32)
    rows = jnp.concatenate([whole[0], sides[0][0]], axis=0)
    bent = [jnp.concatenate([whole[2], sides[0][1]], axis=0)]
    entering = [None, rows]
    for q in range(1, count):
        rows, turned = mm_two(rows, *maps[q][0], *maps[q][2])
        rows = rows + jnp.concatenate([none, sides[q][0]], axis=0)
        bent.append(turned + jnp.concatenate([none, sides[q][1]], axis=0))
        entering.append(rows)
    last = sum(part.astype(f32) for part in maps[-1][1])
    back = jnp.concatenate([bent[-1], last], axis=0)
    leaving = [None] * count
    for q in reversed(range(count - 1)):
        leaving[q] = back
        back = mm_parts(back, *maps[q][1])
        size = bent[q].shape[0]
        back = jnp.concatenate([back[:size] + bent[q], back[size:]], axis=0)
    size = bent[0].shape[0]
    whole = (rows[:B], back[size:], back[:B])
    return whole, (rows[B:], back[B:size]), entering[:count], leaving


def keep_entries(keep_maps, keep, first, entering, leaving, width):
    identity = (
        lax.broadcasted_iota(jnp.int32, (B, B), 0) == lax.broadcasted_iota(jnp.int32, (B, B), 1)
    ).astype(f32)
    none, nothing = jnp.zeros((B, B), f32), jnp.zeros((width, B), f32)
    for q in range(len(entering)):
        f, u = entering[q], leaving[q]
        keep_maps[first + q, 0] = identity if f is None else f[:B]
        keep[first + q, 0] = nothing if f is None else f[B:]
        keep_maps[first + q, 1] = identity if u is None else u[B + width :]
        keep_maps[first + q, 2] = none if u is None else u[:B]
        keep[first + q, 1] = nothing if u is None else u[B : B + width]


def row_solve(maps_hbm, bg_ref, out_ref, xyz_ref, own_ref, maps_ref, sems, keep_maps, keep):
    width = bg_ref.shape[2]
    quads = [pl.ds(8 * h, 8) for h in range(4)]
    copies = start_copies([maps_hbm.at[q] for q in quads], [maps_ref.at[q] for q in quads], sems)
    quad_maps, quad_sides = [], []
    for h in range(4):
        copies[h].wait()
        maps, sides = [], []
        for p in range(4 * h, 4 * h + 4):
            part = [
                jnp.concatenate([maps_ref[2 * p, m], maps_ref[2 * p + 1, m]], axis=0) for m in range(5)
            ]
            maps.append((part[:2], part[2:4], (part[4], None)))
            sides.append([bg_ref[p, m].astype(f32) for m in range(2)])
        quad, side, entering, leaving = compose(maps, sides)
        keep_entries(keep_maps, keep, 4 * h, entering, leaving, width)
        quad_maps.append([split(m) for m in quad])
        quad_sides.append(side)
    row, side, entering, leaving = compose(quad_maps, quad_sides)
    keep_entries(keep_maps, keep, 16, entering, leaving, width)
    sent = map_parts(row)
    sides = split(side[0]) + split(side[1])
    for n in range(out_ref.shape[0]):
        for m in range(5):
            out_ref[n, m * B : (m + 1) * B] = sent[m]
        for m in range(4):
            out_ref[n, 5 * B + m * width : 5 * B + (m + 1) * width] = sides[m]
    high, low = 16 + lax.axis_index("zh"), 4 * lax.axis_index("zh") + lax.axis_index("zl")
    x, y, z = (keep_maps[low, m] for m in range(3))
    f = mm(jnp.concatenate([keep_maps[high, 0], keep[high, 0]], axis=0), x)
    u = mm(jnp.concatenate([keep_maps[high, 2], keep_maps[high, 1], keep[high, 1]], axis=0), y)
    z = mm(jnp.concatenate([keep_maps[high, 0], keep[high, 0]], axis=0), z)
    xyz_ref[0] = f[:B]
    xyz_ref[1] = u[B : 2 * B]
    xyz_ref[2] = u[:B] + z[:B]
    own_ref[0] = f[B:] + keep[low, 0]
    own_ref[1] = u[2 * B :] + z[B:] + keep[low, 1]


def chain(maps, bgs, keep):
    count = len(maps)
    f = bgs[0][0]
    entering = [None, f]
    for q in range(1, count - 1):
        f = mm(f, maps[q][0]) + bgs[q][0]
        entering.append(f)
    turned = [None] + [mm(entering[q], maps[q][2]) + bgs[q][1] for q in range(1, count)]
    keep[0, 0] = jnp.zeros_like(f)
    keep[count - 1, 1] = jnp.zeros_like(f)
    for q in range(1, count):
        keep[q, 0] = entering[q]
    u = turned[-1]
    for q in reversed(range(count - 1)):
        keep[q, 1] = u
        if q > 0:
            u = mm(u, maps[q][1]) + turned[q]


def top_solve(got_ref, xyz_ref, own_ref, wy_ref, local_ref, sep_ref, low_ref, keep):
    width = own_ref.shape[1]
    count = got_ref.shape[0]
    maps, bgs = [], []
    for q in range(count):
        part = [got_ref[q, m * B : (m + 1) * B].astype(f32) for m in range(5)]
        maps.append([part[0] + part[1], part[2] + part[3], part[4]])
        side = [
            got_ref[q, 5 * B + m * width : 5 * B + (m + 1) * width].astype(f32) for m in range(4)
        ]
        bgs.append([side[0] + side[1], side[2] + side[3]])
    chain(maps, bgs, keep)
    f, u = keep[lax.axis_index("row"), 0], keep[lax.axis_index("row"), 1]
    f, u = (
        mm(f, xyz_ref[0]) + own_ref[0],
        mm(u, xyz_ref[1]) + mm(f, xyz_ref[2]) + own_ref[1],
    )
    reached = mm(jnp.concatenate([f, u], axis=1), wy_ref[...])
    for s in range(4):
        value = local_ref[s] + reached[:, s * B : (s + 1) * B]
        sep_ref[s] = value
        low = value.astype(bf16)
        for n in range(low_ref.shape[0]):
            low_ref[n, s] = low


def join_upper(upper_ref, inv_ref, out_ref):
    for k in range(2):
        for i in range(4):
            out_ref[k, i * B : (i + 1) * B] = upper_ref[k, i].astype(f32).T.astype(bf16)
        out_ref[k, 4 * B :] = inv_ref[k].astype(f32).T.astype(bf16)


def leaf_backward(place_ref, solved_ref, forward_ref, upper_ref, out_ref):
    for j in range(out_ref.shape[0]):
        for k in range(2):
            solved = [solved_ref[place_ref[j, 4 * k + i]] for i in range(4)]
            total = dot(jnp.concatenate(solved, axis=1), upper_ref[j, k, : 4 * B])
            residual = (forward_ref[j, k].astype(f32) - total).astype(bf16)
            out_ref[j, k] = dot(residual, upper_ref[j, k, 4 * B :]).astype(bf16)


def turn_leaf(got_ref, out_ref):
    width = got_ref.shape[2]
    for k in range(2):
        whole = jnp.concatenate([got_ref[j, k] for j in range(got_ref.shape[0])], axis=0)
        out_ref[k] = whole.astype(f32).T.astype(bf16)


def turn_sep(place_ref, got_ref, out_ref, pass_ref):
    pass_ref[...] = place_ref[...]
    for k in range(2):
        s = 2 * lax.axis_index("core") + k
        whole = jnp.concatenate([got_ref[j, s] for j in range(got_ref.shape[0])], axis=0)
        out_ref[k] = whole.T


def exchange(value, axes):
    return lax.all_to_all(value, axes, split_axis=0, concat_axis=0, tiled=True)


def on_device(
    leaf_rhs,
    leaf_lower_inv,
    leaf_upper_inv,
    leaf_lower,
    leaf_upper,
    targets,
    sep_rhs,
    sep_lower_inv,
    sep_upper_inv,
    sep_lower_link,
    sep_upper_link,
):
    across = ("layer", "core")
    layers, rows = lax.axis_size("layer"), lax.axis_size("row")
    highs, lows = lax.axis_size("zh"), lax.axis_size("zl")
    groups = 2 * layers
    width = 256 // groups
    chips = highs * lows

    along = ("zh", "zl")
    pair = (2, width, B)

    sources = (sep_lower_inv, sep_lower_link, sep_upper_inv, sep_upper_link, sep_rhs)
    blocks = shaped((2, 4 * B + width, B), f32)
    half_maps = shaped((5, B // 2, B), bf16)
    maps = shaped((3, B, B), f32)
    mine, others = call(
        sep_prepare,
        (blocks, blocks),
        landing(sources) + [pltpu.VMEM((2, 256, B), f32)],
        "sep_prepare",
        hbm=range(0, 5),
        limit=VMEM_ALL,
    )(*sources)
    theirs = lax.ppermute(others, "core", [(0, 1), (1, 0)])

    sources = (leaf_rhs, leaf_lower_inv, leaf_lower)
    sent = call(
        leaf_forward,
        shaped((groups, 10 * width + 16, B), bf16),
        landing(sources),
        "leaf_forward",
        smem=(0,),
        hbm=(1, 2, 3),
        limit=VMEM_ALL,
        after=(mine,),
    )(targets, *sources)
    seps, half, wy = call(
        chip_maps,
        (shaped((2, 2, 4 * B + width, B), f32), half_maps, shaped((2 * B, 4 * B), f32)),
        [pltpu.VMEM((5, B, B), bf16)],
        "chip_maps",
        limit=VMEM_ALL,
        after=(sent,),
    )(mine, theirs)
    by_chip = lax.all_gather(half, along + ("core",)).reshape((2 * chips,) + half_maps.shape)

    got = exchange(sent, across)
    place = got[:, 10 * width, :8].astype(jnp.int32)
    sums, forward = call(
        scatter_updates,
        (shaped((chips, 4, width, B), bf16), shaped((groups, 2, width, B), bf16)),
        [pltpu.VMEM((4 * chips, width, B), f32)],
        "scatter_updates",
        smem=(0,),
    )(place, got)

    bg, local = call(
        chip_solve, (shaped((chips,) + pair, bf16), shaped((4, width, B), f32)), name="chip_solve"
    )(exchange(sums, along), seps)
    sent_on, xyz, own = call(
        row_solve,
        (shaped((rows, 5 * B + 4 * width, B), bf16), maps, shaped(pair, f32)),
        [
            pltpu.VMEM((2 * chips,) + half_maps.shape, bf16),
            pltpu.SemaphoreType.DMA((4,)),
            pltpu.VMEM((20, 3, B, B), f32),
            pltpu.VMEM((20,) + pair, f32),
        ],
        "row_solve",
        hbm=(0,),
        limit=VMEM_ALL,
    )(by_chip, exchange(bg, along))
    solved, solved_low = call(
        top_solve,
        (shaped((4, width, B), f32), shaped((chips, 4, width, B), bf16)),
        [pltpu.VMEM((rows,) + pair, f32)],
        "top_solve",
        limit=VMEM_ALL,
    )(exchange(sent_on, "row"), xyz, own, wy, local)

    joined = call(
        join_upper, shaped((2, 5 * B, B), bf16), name="join_upper", after=(sums,), limit=VMEM_ALL
    )(leaf_upper, leaf_upper_inv)
    upper = lax.all_gather(joined, across).reshape((groups, 2, 5 * B, B))
    low = exchange(solved_low, along).reshape(4 * chips, width, B)
    sep_all = lax.all_gather(solved, across).reshape((groups, 4, width, B))
    sep_part, place = call(
        turn_sep,
        (shaped((2, B, 256), f32), shaped(place.shape, jnp.int32)),
        name="turn_sep",
        after=(upper,),
    )(place, sep_all)
    back = call(
        leaf_backward,
        shaped((groups, 2, width, B), bf16),
        name="leaf_backward",
        smem=(0,),
    )(place, low, forward, upper)
    leaf_part = call(turn_leaf, shaped((2, B, 256), bf16), name="turn_leaf")(exchange(back, across))
    return (leaf_part, sep_part)


def solution(mesh):
    layers, rows, cols = (mesh.shape[name] for name in ("layer", "row", "col"))
    lows = 4
    fine = Mesh(
        mesh.devices.reshape(layers, rows, cols // (2 * lows), lows, 2),
        ("layer", "row", "zh", "zl", "core"),
    )
    leaf = ("layer", "row", "zh", "zl", "core")
    sep = ("row", "zh", "zl", "core")
    return jax.shard_map(
        on_device,
        mesh=fine,
        in_specs=(P(leaf),) * 6 + (P(sep),) * 5,
        out_specs=(P(leaf), P(sep)),
        check_vma=False,
    )
```

```python
import jax
import jax.numpy as jnp
from jax import lax
from jax.experimental import pallas as pl
from jax.experimental.pallas import tpu as pltpu
from jax.sharding import Mesh
from jax.sharding import PartitionSpec as P

f32 = jnp.float32
bf16 = jnp.bfloat16

B = 128
VMEM_LIMIT = 16 * 1024 * 1024
VMEM_ALL = 60 * 1024 * 1024


def dot(a, b):
    return jnp.dot(a, b, preferred_element_type=f32)


def dot_nt(a, b):
    return lax.dot_general(a, b, (((1,), (1,)), ((), ())), preferred_element_type=f32)


def split(x):
    high = x.astype(bf16)
    return high, (x - high.astype(f32)).astype(bf16)


def mm(a, b):
    a_high, a_low = split(a)
    b_high, b_low = split(b)
    if b.shape == (B, B):
        wide = jnp.concatenate([b_high, b_low], axis=1)
        parts = dot(jnp.concatenate([a_high, a_low], axis=1), jnp.concatenate([wide, wide], axis=0))
        return parts[:, :B] + parts[:, B:]
    return dot(a_high, b_high) + (dot(a_low, b_high) + dot(a_high, b_low))


def call(kernel, outs, scratch=(), name=None, smem=(), hbm=(), after=(), limit=VMEM_LIMIT):
    def run(*operands):
        count = len(operands)

        def body(*refs):
            kernel(*refs[:count], *refs[count + len(after) :])

        def space(k):
            return pltpu.SMEM if k in smem else pltpu.HBM if k in hbm else pltpu.VMEM

        return pl.pallas_call(
            body,
            out_shape=outs,
            in_specs=[pl.BlockSpec(memory_space=space(k)) for k in range(count)]
            + [pl.BlockSpec(memory_space=pl.ANY)] * len(after),
            out_specs=jax.tree.map(lambda _: pl.BlockSpec(memory_space=pltpu.VMEM), outs),
            scratch_shapes=list(scratch),
            compiler_params=pltpu.CompilerParams(vmem_limit_bytes=limit),
            name=name,
        )(*operands, *after)

    return run


def landing(arrays):
    return [pltpu.VMEM(x.shape, x.dtype) for x in arrays] + [pltpu.SemaphoreType.DMA((len(arrays),))]


def start_copies(sources, targets, sems):
    copies = [
        pltpu.make_async_copy(source, target, sems.at[k])
        for k, (source, target) in enumerate(zip(sources, targets))
    ]
    for copy in copies:
        copy.start()
    return copies


def shaped(shape, dtype):
    return jax.ShapeDtypeStruct(shape, dtype)


def scatter_updates(place_ref, got_ref, out_ref, forward_ref, total):
    width = out_ref.shape[-2]
    total[...] = jnp.zeros_like(total)
    for j in range(got_ref.shape[0]):
        for slot in range(8):
            s = place_ref[j, slot]
            total[s] = total[s] + got_ref[j, slot * width : (slot + 1) * width].astype(f32)
    out_ref[...] = total[...].reshape(out_ref.shape).astype(bf16)
    for k in range(2):
        forward_ref[:, k] = got_ref[:, (8 + k) * width : (9 + k) * width]


def leaf_forward(tgt_ref, *refs):
    sources, sent_ref, landed, sems = refs[:3], refs[3], refs[4:7], refs[7]
    copies = start_copies(sources, landed, sems)
    rhs_ref, inv_ref, lower_ref = landed
    groups = sent_ref.shape[0]
    width = 256 // groups
    lane = lax.broadcasted_iota(jnp.int32, (16, B), 1)
    places = jnp.zeros((16, B), jnp.int32)
    for slot in range(8):
        places = jnp.where(lane == slot, tgt_ref[slot // 4, slot % 4], places)
    for j in range(groups):
        sent_ref[j, 10 * width :] = places.astype(f32).astype(bf16)
    copies[0].wait()
    copies[1].wait()
    forwards = []
    for k in range(2):
        forward = dot(inv_ref[k], rhs_ref[k]).T.astype(bf16)
        forwards.append(forward)
        for j in range(groups):
            sent_ref[j, (8 + k) * width : (9 + k) * width] = forward[j * width : (j + 1) * width]
    copies[2].wait()
    for k in range(2):
        for i in range(4):
            update = dot_nt(forwards[k], lower_ref[k, i]).astype(bf16)
            slot = 4 * k + i
            for j in range(groups):
                sent_ref[j, slot * width : (slot + 1) * width] = update[j * width : (j + 1) * width]


def sep_prepare(*refs):
    sources, (mine_ref, other_ref), landed, sems, turned = refs[:5], refs[5:7], refs[7:12], refs[12], refs[13]
    copies = start_copies(sources, landed, sems)
    li_ref, ll_ref, ui_ref, ul_ref, rhs_ref = landed
    width = mine_ref.shape[1] - 4 * B
    for copy in copies:
        copy.wait()
    for s in range(2):
        turned[s] = rhs_ref[s].T
        li, ui = li_ref[s], ui_ref[s]
        blocks = (-mm(li, ll_ref[s]).T, -mm(ui, ul_ref[s]).T, li.T, ui.T)
        for ref, core in ((mine_ref, lax.axis_index("core")), (other_ref, 1 - lax.axis_index("core"))):
            for k in range(4):
                ref[s, k * B : (k + 1) * B] = blocks[k]
            first = pl.multiple_of((2 * lax.axis_index("layer") + core) * width, width)
            ref[s, 4 * B :] = turned[s, pl.ds(first, width)]


def map_parts(maps):
    return split(maps[0]) + split(maps[1]) + (maps[2].astype(bf16),)


def send_half(maps, half_ref, whole):
    for m, part in enumerate(map_parts(maps)):
        whole[m] = part
    half_ref[...] = whole[:, pl.ds(pl.multiple_of(lax.axis_index("core") * (B // 2), B // 2), B // 2)]


def chip_dependence(mine_ref, other_ref, sep_ref):
    sep_ref[lax.axis_index("core")] = mine_ref[...]
    sep_ref[1 - lax.axis_index("core")] = other_ref[...]

    def block(s, k):
        return sep_ref[s // 2, s % 2, k * B : (k + 1) * B]

    reach = [block(0, 0)]
    for s in range(1, 4):
        reach.append(mm(reach[-1], block(s, 0)))
    wy = jnp.concatenate([mm(reach[3], block(3, 3)), block(3, 1)], axis=0)
    wys = [wy]
    for s in (2, 1, 0):
        wy = mm(wy, block(s, 1))
        wy = jnp.concatenate([wy[:B] + mm(reach[s], block(s, 3)), wy[B:]], axis=0)
        wys.insert(0, wy)
    return reach[3], wys


def chip_maps(mine_ref, other_ref, half_ref, whole, seps):
    reach, wys = chip_dependence(mine_ref, other_ref, seps)
    send_half((reach, wys[0][B:], wys[0][:B]), half_ref, whole)


def chip_entries(mine_ref, other_ref, half_ref, sep_ref, wy_ref):
    _, wys = chip_dependence(mine_ref, other_ref, sep_ref)
    for s in range(4):
        wy_ref[:, s * B : (s + 1) * B] = wys[s]


def chip_solve(got_ref, sep_ref, bg_ref, local_ref):
    total = jnp.sum(got_ref[...].astype(f32), axis=0)

    def block(s, k):
        return sep_ref[s // 2, s % 2, k * B : (k + 1) * B]

    base = [
        mm(sep_ref[s // 2, s % 2, 4 * B :] - total[s], block(s, 2)) for s in range(4)
    ]
    f = base[0]
    forward = [f]
    for s in range(1, 4):
        f = mm(f, block(s, 0)) + base[s]
        forward.append(f)
    bent = [mm(forward[s], block(s, 3)) for s in range(4)]
    u = bent[3]
    local_ref[3] = u
    for s in (2, 1, 0):
        u = mm(u, block(s, 1)) + bent[s]
        local_ref[s] = u
    for n in range(bg_ref.shape[0]):
        bg_ref[n, 0] = f.astype(bf16)
        bg_ref[n, 1] = u.astype(bf16)


def mm_parts(a, high, low):
    a_high, a_low = split(a)
    wide = jnp.concatenate([high, low], axis=1)
    parts = dot(jnp.concatenate([a_high, a_low], axis=1), jnp.concatenate([wide, wide], axis=0))
    return parts[:, :B] + parts[:, B:]


def mm_two(a, b_high, b_low, c_high, c_low):
    a_high, a_low = split(a)
    high = jnp.concatenate([b_high, c_high], axis=1)
    both = dot(jnp.concatenate([a_high, a_low], axis=1), jnp.concatenate([high, high], axis=0))
    if c_low is None:
        return both[:, :B] + dot(a_high, b_low), both[:, B:]
    both = both + dot(a_high, jnp.concatenate([b_low, c_low], axis=1))
    return both[:, :B], both[:, B:]


def compose(maps, sides):
    count = len(maps)
    whole = [sum(part.astype(f32) for part in m if part is not None) for m in maps[0]]
    none = jnp.zeros((B, B), f32)
    rows = jnp.concatenate([whole[0], sides[0][0]], axis=0)
    bent = [jnp.concatenate([whole[2], sides[0][1]], axis=0)]
    entering = [None, rows]
    for q in range(1, count):
        rows, turned = mm_two(rows, *maps[q][0], *maps[q][2])
        rows = rows + jnp.concatenate([none, sides[q][0]], axis=0)
        bent.append(turned + jnp.concatenate([none, sides[q][1]], axis=0))
        entering.append(rows)
    last = sum(part.astype(f32) for part in maps[-1][1])
    back = jnp.concatenate([bent[-1], last], axis=0)
    leaving = [None] * count
    for q in reversed(range(count - 1)):
        leaving[q] = back
        back = mm_parts(back, *maps[q][1])
        size = bent[q].shape[0]
        back = jnp.concatenate([back[:size] + bent[q], back[size:]], axis=0)
    size = bent[0].shape[0]
    whole = (rows[:B], back[size:], back[:B])
    return whole, (rows[B:], back[B:size]), entering[:count], leaving


def keep_entries(keep_maps, keep, first, entering, leaving, width):
    identity = (
        lax.broadcasted_iota(jnp.int32, (B, B), 0) == lax.broadcasted_iota(jnp.int32, (B, B), 1)
    ).astype(f32)
    none, nothing = jnp.zeros((B, B), f32), jnp.zeros((width, B), f32)
    for q in range(len(entering)):
        f, u = entering[q], leaving[q]
        keep_maps[first + q, 0] = identity if f is None else f[:B]
        keep[first + q, 0] = nothing if f is None else f[B:]
        keep_maps[first + q, 1] = identity if u is None else u[B + width :]
        keep_maps[first + q, 2] = none if u is None else u[:B]
        keep[first + q, 1] = nothing if u is None else u[B : B + width]


def row_solve(maps_hbm, bg_ref, out_ref, xyz_ref, own_ref, maps_ref, sems, keep_maps, keep):
    width = bg_ref.shape[2]
    quads = [pl.ds(8 * h, 8) for h in range(4)]
    copies = start_copies([maps_hbm.at[q] for q in quads], [maps_ref.at[q] for q in quads], sems)
    quad_maps, quad_sides = [], []
    for h in range(4):
        copies[h].wait()
        maps, sides = [], []
        for p in range(4 * h, 4 * h + 4):
            part = [
                jnp.concatenate([maps_ref[2 * p, m], maps_ref[2 * p + 1, m]], axis=0) for m in range(5)
            ]
            maps.append((part[:2], part[2:4], (part[4], None)))
            sides.append([bg_ref[p, m].astype(f32) for m in range(2)])
        quad, side, entering, leaving = compose(maps, sides)
        keep_entries(keep_maps, keep, 4 * h, entering, leaving, width)
        quad_maps.append([split(m) for m in quad])
        quad_sides.append(side)
    row, side, entering, leaving = compose(quad_maps, quad_sides)
    keep_entries(keep_maps, keep, 16, entering, leaving, width)
    sent = [part.astype(bf16) for part in row]
    sides = split(side[0]) + split(side[1])
    for n in range(out_ref.shape[0]):
        for m in range(3):
            out_ref[n, m * B : (m + 1) * B] = sent[m]
        for m in range(4):
            out_ref[n, 3 * B + m * width : 3 * B + (m + 1) * width] = sides[m]
    high, low = 16 + lax.axis_index("zh"), 4 * lax.axis_index("zh") + lax.axis_index("zl")
    x, y, z = (keep_maps[low, m] for m in range(3))
    f = mm(jnp.concatenate([keep_maps[high, 0], keep[high, 0]], axis=0), x)
    u = mm(jnp.concatenate([keep_maps[high, 2], keep_maps[high, 1], keep[high, 1]], axis=0), y)
    z = mm(jnp.concatenate([keep_maps[high, 0], keep[high, 0]], axis=0), z)
    xyz_ref[0] = f[:B]
    xyz_ref[1] = u[B : 2 * B]
    xyz_ref[2] = u[:B] + z[:B]
    own_ref[0] = f[B:] + keep[low, 0]
    own_ref[1] = u[2 * B :] + z[B:] + keep[low, 1]


def chain(maps, bgs, keep):
    count = len(maps)
    f = bgs[0][0]
    entering = [None, f]
    for q in range(1, count - 1):
        f = mm(f, maps[q][0]) + bgs[q][0]
        entering.append(f)
    turned = [None] + [mm(entering[q], maps[q][2]) + bgs[q][1] for q in range(1, count)]
    keep[0, 0] = jnp.zeros_like(f)
    keep[count - 1, 1] = jnp.zeros_like(f)
    for q in range(1, count):
        keep[q, 0] = entering[q]
    u = turned[-1]
    for q in reversed(range(count - 1)):
        keep[q, 1] = u
        if q > 0:
            u = mm(u, maps[q][1]) + turned[q]


def top_solve(got_ref, xyz_ref, own_ref, wy_ref, local_ref, sep_ref, low_ref, keep):
    width = own_ref.shape[1]
    count = got_ref.shape[0]
    maps, bgs = [], []
    for q in range(count):
        maps.append([got_ref[q, m * B : (m + 1) * B].astype(f32) for m in range(3)])
        side = [
            got_ref[q, 3 * B + m * width : 3 * B + (m + 1) * width].astype(f32) for m in range(4)
        ]
        bgs.append([side[0] + side[1], side[2] + side[3]])
    chain(maps, bgs, keep)
    f, u = keep[lax.axis_index("row"), 0], keep[lax.axis_index("row"), 1]
    f, u = (
        mm(f, xyz_ref[0]) + own_ref[0],
        mm(u, xyz_ref[1]) + mm(f, xyz_ref[2]) + own_ref[1],
    )
    reached = mm(jnp.concatenate([f, u], axis=1), wy_ref[...])
    for s in range(4):
        value = local_ref[s] + reached[:, s * B : (s + 1) * B]
        sep_ref[s] = value
        low = value.astype(bf16)
        for n in range(low_ref.shape[0]):
            low_ref[n, s] = low


def join_upper(upper_ref, inv_ref, out_ref):
    for k in range(2):
        for i in range(4):
            out_ref[k, i * B : (i + 1) * B] = upper_ref[k, i].astype(f32).T.astype(bf16)
        out_ref[k, 4 * B :] = inv_ref[k].astype(f32).T.astype(bf16)


def leaf_backward(place_ref, solved_ref, forward_ref, upper_ref, out_ref):
    for j in range(out_ref.shape[0]):
        for k in range(2):
            solved = [solved_ref[place_ref[j, 4 * k + i]] for i in range(4)]
            total = dot(jnp.concatenate(solved, axis=1), upper_ref[j, k, : 4 * B])
            residual = (forward_ref[j, k].astype(f32) - total).astype(bf16)
            out_ref[j, k] = dot(residual, upper_ref[j, k, 4 * B :]).astype(bf16)


def turn_leaf(got_ref, out_ref):
    width = got_ref.shape[2]
    for k in range(2):
        whole = jnp.concatenate([got_ref[j, k] for j in range(got_ref.shape[0])], axis=0)
        out_ref[k] = whole.astype(f32).T.astype(bf16)


def turn_sep(place_ref, got_ref, out_ref, pass_ref):
    pass_ref[...] = place_ref[...]
    for k in range(2):
        s = 2 * lax.axis_index("core") + k
        whole = jnp.concatenate([got_ref[j, s] for j in range(got_ref.shape[0])], axis=0)
        out_ref[k] = whole.T


def exchange(value, axes):
    return lax.all_to_all(value, axes, split_axis=0, concat_axis=0, tiled=True)


def on_device(
    leaf_rhs,
    leaf_lower_inv,
    leaf_upper_inv,
    leaf_lower,
    leaf_upper,
    targets,
    sep_rhs,
    sep_lower_inv,
    sep_upper_inv,
    sep_lower_link,
    sep_upper_link,
):
    across = ("layer", "core")
    layers, rows = lax.axis_size("layer"), lax.axis_size("row")
    highs, lows = lax.axis_size("zh"), lax.axis_size("zl")
    groups = 2 * layers
    width = 256 // groups
    chips = highs * lows

    along = ("zh", "zl")
    pair = (2, width, B)

    sources = (sep_lower_inv, sep_lower_link, sep_upper_inv, sep_upper_link, sep_rhs)
    blocks = shaped((2, 4 * B + width, B), f32)
    half_maps = shaped((5, B // 2, B), bf16)
    maps = shaped((3, B, B), f32)
    mine, others = call(
        sep_prepare,
        (blocks, blocks),
        landing(sources) + [pltpu.VMEM((2, 256, B), f32)],
        "sep_prepare",
        hbm=range(0, 5),
        limit=VMEM_ALL,
    )(*sources)
    theirs = lax.ppermute(others, "core", [(0, 1), (1, 0)])

    sources = (leaf_rhs, leaf_lower_inv, leaf_lower)
    sent = call(
        leaf_forward,
        shaped((groups, 10 * width + 16, B), bf16),
        landing(sources),
        "leaf_forward",
        smem=(0,),
        hbm=(1, 2, 3),
        limit=VMEM_ALL,
        after=(mine,),
    )(targets, *sources)
    half = call(
        chip_maps,
        half_maps,
        [pltpu.VMEM((5, B, B), bf16), pltpu.VMEM((2, 2, 4 * B + width, B), f32)],
        "chip_maps",
        limit=VMEM_ALL,
        after=(sent,),
    )(mine, theirs)
    seps, wy = call(
        chip_entries,
        (shaped((2, 2, 4 * B + width, B), f32), shaped((2 * B, 4 * B), f32)),
        name="chip_entries",
        limit=VMEM_ALL,
    )(mine, theirs, half)
    by_chip = lax.all_gather(half, along + ("core",)).reshape((2 * chips,) + half_maps.shape)

    got = exchange(sent, across)
    place = got[:, 10 * width, :8].astype(jnp.int32)
    sums, forward = call(
        scatter_updates,
        (shaped((chips, 4, width, B), bf16), shaped((groups, 2, width, B), bf16)),
        [pltpu.VMEM((4 * chips, width, B), f32)],
        "scatter_updates",
        smem=(0,),
    )(place, got)

    bg, local = call(
        chip_solve, (shaped((chips,) + pair, bf16), shaped((4, width, B), f32)), name="chip_solve"
    )(exchange(sums, along), seps)
    sent_on, xyz, own = call(
        row_solve,
        (shaped((rows, 3 * B + 4 * width, B), bf16), maps, shaped(pair, f32)),
        [
            pltpu.VMEM((2 * chips,) + half_maps.shape, bf16),
            pltpu.SemaphoreType.DMA((4,)),
            pltpu.VMEM((20, 3, B, B), f32),
            pltpu.VMEM((20,) + pair, f32),
        ],
        "row_solve",
        hbm=(0,),
        limit=VMEM_ALL,
    )(by_chip, exchange(bg, along))
    solved, solved_low = call(
        top_solve,
        (shaped((4, width, B), f32), shaped((chips, 4, width, B), bf16)),
        [pltpu.VMEM((rows,) + pair, f32)],
        "top_solve",
        limit=VMEM_ALL,
    )(exchange(sent_on, "row"), xyz, own, wy, local)

    joined = call(
        join_upper, shaped((2, 5 * B, B), bf16), name="join_upper", after=(sums,), limit=VMEM_ALL
    )(leaf_upper, leaf_upper_inv)
    upper = lax.all_gather(joined, across).reshape((groups, 2, 5 * B, B))
    low = exchange(solved_low, along).reshape(4 * chips, width, B)
    sep_all = lax.all_gather(solved, across).reshape((groups, 4, width, B))
    sep_part, place = call(
        turn_sep,
        (shaped((2, B, 256), f32), shaped(place.shape, jnp.int32)),
        name="turn_sep",
        after=(upper,),
    )(place, sep_all)
    back = call(
        leaf_backward,
        shaped((groups, 2, width, B), bf16),
        name="leaf_backward",
        smem=(0,),
    )(place, low, forward, upper)
    leaf_part = call(turn_leaf, shaped((2, B, 256), bf16), name="turn_leaf")(exchange(back, across))
    return (leaf_part, sep_part)


def solution(mesh):
    layers, rows, cols = (mesh.shape[name] for name in ("layer", "row", "col"))
    lows = 4
    fine = Mesh(
        mesh.devices.reshape(layers, rows, cols // (2 * lows), lows, 2),
        ("layer", "row", "zh", "zl", "core"),
    )
    leaf = ("layer", "row", "zh", "zl", "core")
    sep = ("row", "zh", "zl", "core")
    return jax.shard_map(
        on_device,
        mesh=fine,
        in_specs=(P(leaf),) * 6 + (P(sep),) * 5,
        out_specs=(P(leaf), P(sep)),
        check_vma=False,
    )
```

```python
import jax
import jax.numpy as jnp
from jax import lax
from jax.experimental import pallas as pl
from jax.experimental.pallas import tpu as pltpu
from jax.sharding import Mesh
from jax.sharding import PartitionSpec as P

f32 = jnp.float32
bf16 = jnp.bfloat16

B = 128
VMEM_LIMIT = 16 * 1024 * 1024
VMEM_ALL = 60 * 1024 * 1024


def dot(a, b):
    return jnp.dot(a, b, preferred_element_type=f32)


def dot_nt(a, b):
    return lax.dot_general(a, b, (((1,), (1,)), ((), ())), preferred_element_type=f32)


def split(x):
    high = x.astype(bf16)
    return high, (x - high.astype(f32)).astype(bf16)


def mm(a, b):
    a_high, a_low = split(a)
    b_high, b_low = split(b)
    if b.shape == (B, B):
        wide = jnp.concatenate([b_high, b_low], axis=1)
        parts = dot(jnp.concatenate([a_high, a_low], axis=1), jnp.concatenate([wide, wide], axis=0))
        return parts[:, :B] + parts[:, B:]
    return dot(a_high, b_high) + (dot(a_low, b_high) + dot(a_high, b_low))


def call(kernel, outs, scratch=(), name=None, smem=(), hbm=(), after=(), limit=VMEM_LIMIT):
    def run(*operands):
        count = len(operands)

        def body(*refs):
            kernel(*refs[:count], *refs[count + len(after) :])

        def space(k):
            return pltpu.SMEM if k in smem else pltpu.HBM if k in hbm else pltpu.VMEM

        return pl.pallas_call(
            body,
            out_shape=outs,
            in_specs=[pl.BlockSpec(memory_space=space(k)) for k in range(count)]
            + [pl.BlockSpec(memory_space=pl.ANY)] * len(after),
            out_specs=jax.tree.map(lambda _: pl.BlockSpec(memory_space=pltpu.VMEM), outs),
            scratch_shapes=list(scratch),
            compiler_params=pltpu.CompilerParams(vmem_limit_bytes=limit),
            name=name,
        )(*operands, *after)

    return run


def landing(arrays):
    return [pltpu.VMEM(x.shape, x.dtype) for x in arrays] + [pltpu.SemaphoreType.DMA((len(arrays),))]


def start_copies(sources, targets, sems):
    copies = [
        pltpu.make_async_copy(source, target, sems.at[k])
        for k, (source, target) in enumerate(zip(sources, targets))
    ]
    for copy in copies:
        copy.start()
    return copies


def shaped(shape, dtype):
    return jax.ShapeDtypeStruct(shape, dtype)


def scatter_updates(place_ref, got_ref, out_ref, forward_ref, total):
    width = out_ref.shape[-2]
    total[...] = jnp.zeros_like(total)
    for j in range(got_ref.shape[0]):
        for slot in range(8):
            s = place_ref[j, slot]
            total[s] = total[s] + got_ref[j, slot * width : (slot + 1) * width].astype(f32)
    out_ref[...] = total[...].reshape(out_ref.shape).astype(bf16)
    for k in range(2):
        forward_ref[:, k] = got_ref[:, (8 + k) * width : (9 + k) * width]


def leaf_forward(tgt_ref, *refs):
    sources, sent_ref, landed, sems = refs[:3], refs[3], refs[4:7], refs[7]
    copies = start_copies(sources, landed, sems)
    rhs_ref, inv_ref, lower_ref = landed
    groups = sent_ref.shape[0]
    width = 256 // groups
    lane = lax.broadcasted_iota(jnp.int32, (16, B), 1)
    places = jnp.zeros((16, B), jnp.int32)
    for slot in range(8):
        places = jnp.where(lane == slot, tgt_ref[slot // 4, slot % 4], places)
    for j in range(groups):
        sent_ref[j, 10 * width :] = places.astype(f32).astype(bf16)
    copies[0].wait()
    copies[1].wait()
    forwards = []
    for k in range(2):
        forward = dot(inv_ref[k], rhs_ref[k]).T.astype(bf16)
        forwards.append(forward)
        for j in range(groups):
            sent_ref[j, (8 + k) * width : (9 + k) * width] = forward[j * width : (j + 1) * width]
    copies[2].wait()
    for k in range(2):
        for i in range(4):
            update = dot_nt(forwards[k], lower_ref[k, i]).astype(bf16)
            slot = 4 * k + i
            for j in range(groups):
                sent_ref[j, slot * width : (slot + 1) * width] = update[j * width : (j + 1) * width]


def sep_prepare(*refs):
    sources, (mine_ref, other_ref), landed, sems, turned = refs[:5], refs[5:7], refs[7:12], refs[12], refs[13]
    copies = start_copies(sources, landed, sems)
    li_ref, ll_ref, ui_ref, ul_ref, rhs_ref = landed
    width = mine_ref.shape[1] - 4 * B
    for copy in copies:
        copy.wait()
    for s in range(2):
        turned[s] = rhs_ref[s].T
        li, ui = li_ref[s], ui_ref[s]
        blocks = (-mm(li, ll_ref[s]).T, -mm(ui, ul_ref[s]).T, li.T, ui.T)
        for ref, core in ((mine_ref, lax.axis_index("core")), (other_ref, 1 - lax.axis_index("core"))):
            for k in range(4):
                ref[s, k * B : (k + 1) * B] = blocks[k]
            first = pl.multiple_of((2 * lax.axis_index("layer") + core) * width, width)
            ref[s, 4 * B :] = turned[s, pl.ds(first, width)]


def map_parts(maps):
    return split(maps[0]) + split(maps[1]) + (maps[2].astype(bf16),)


def send_half(maps, half_ref, whole):
    for m, part in enumerate(map_parts(maps)):
        whole[m] = part
    half_ref[...] = whole[:, pl.ds(pl.multiple_of(lax.axis_index("core") * (B // 2), B // 2), B // 2)]


def chip_dependence(mine_ref, other_ref, sep_ref):
    sep_ref[lax.axis_index("core")] = mine_ref[...]
    sep_ref[1 - lax.axis_index("core")] = other_ref[...]

    def block(s, k):
        return sep_ref[s // 2, s % 2, k * B : (k + 1) * B]

    reach = [block(0, 0)]
    for s in range(1, 4):
        reach.append(mm(reach[-1], block(s, 0)))
    wy = jnp.concatenate([mm(reach[3], block(3, 3)), block(3, 1)], axis=0)
    wys = [wy]
    for s in (2, 1, 0):
        wy = mm(wy, block(s, 1))
        wy = jnp.concatenate([wy[:B] + mm(reach[s], block(s, 3)), wy[B:]], axis=0)
        wys.insert(0, wy)
    return reach[3], wys


def chip_maps(mine_ref, other_ref, half_ref, whole, seps):
    reach, wys = chip_dependence(mine_ref, other_ref, seps)
    send_half((reach, wys[0][B:], wys[0][:B]), half_ref, whole)


def chip_entries(mine_ref, other_ref, half_ref, wy_ref, seps):
    _, wys = chip_dependence(mine_ref, other_ref, seps)
    for s in range(4):
        wy_ref[:, s * B : (s + 1) * B] = wys[s]


def chip_solve(got_ref, mine_ref, other_ref, bg_ref, local_ref, sep_ref):
    sep_ref[lax.axis_index("core")] = mine_ref[...]
    sep_ref[1 - lax.axis_index("core")] = other_ref[...]
    total = jnp.sum(got_ref[...].astype(f32), axis=0)

    def block(s, k):
        return sep_ref[s // 2, s % 2, k * B : (k + 1) * B]

    base = [
        mm(sep_ref[s // 2, s % 2, 4 * B :] - total[s], block(s, 2)) for s in range(4)
    ]
    f = base[0]
    forward = [f]
    for s in range(1, 4):
        f = mm(f, block(s, 0)) + base[s]
        forward.append(f)
    bent = [mm(forward[s], block(s, 3)) for s in range(4)]
    u = bent[3]
    local_ref[3] = u
    for s in (2, 1, 0):
        u = mm(u, block(s, 1)) + bent[s]
        local_ref[s] = u
    for n in range(bg_ref.shape[0]):
        bg_ref[n, 0] = f.astype(bf16)
        bg_ref[n, 1] = u.astype(bf16)


def mm_parts(a, high, low):
    a_high, a_low = split(a)
    wide = jnp.concatenate([high, low], axis=1)
    parts = dot(jnp.concatenate([a_high, a_low], axis=1), jnp.concatenate([wide, wide], axis=0))
    return parts[:, :B] + parts[:, B:]


def mm_two(a, b_high, b_low, c_high, c_low):
    a_high, a_low = split(a)
    high = jnp.concatenate([b_high, c_high], axis=1)
    both = dot(jnp.concatenate([a_high, a_low], axis=1), jnp.concatenate([high, high], axis=0))
    if c_low is None:
        return both[:, :B] + dot(a_high, b_low), both[:, B:]
    both = both + dot(a_high, jnp.concatenate([b_low, c_low], axis=1))
    return both[:, :B], both[:, B:]


def compose(maps, sides):
    count = len(maps)
    whole = [sum(part.astype(f32) for part in m if part is not None) for m in maps[0]]
    none = jnp.zeros((B, B), f32)
    rows = jnp.concatenate([whole[0], sides[0][0]], axis=0)
    bent = [jnp.concatenate([whole[2], sides[0][1]], axis=0)]
    entering = [None, rows]
    for q in range(1, count):
        rows, turned = mm_two(rows, *maps[q][0], *maps[q][2])
        rows = rows + jnp.concatenate([none, sides[q][0]], axis=0)
        bent.append(turned + jnp.concatenate([none, sides[q][1]], axis=0))
        entering.append(rows)
    last = sum(part.astype(f32) for part in maps[-1][1])
    back = jnp.concatenate([bent[-1], last], axis=0)
    leaving = [None] * count
    for q in reversed(range(count - 1)):
        leaving[q] = back
        back = mm_parts(back, *maps[q][1])
        size = bent[q].shape[0]
        back = jnp.concatenate([back[:size] + bent[q], back[size:]], axis=0)
    size = bent[0].shape[0]
    whole = (rows[:B], back[size:], back[:B])
    return whole, (rows[B:], back[B:size]), entering[:count], leaving


def keep_entries(keep_maps, keep, first, entering, leaving, width):
    identity = (
        lax.broadcasted_iota(jnp.int32, (B, B), 0) == lax.broadcasted_iota(jnp.int32, (B, B), 1)
    ).astype(f32)
    none, nothing = jnp.zeros((B, B), f32), jnp.zeros((width, B), f32)
    for q in range(len(entering)):
        f, u = entering[q], leaving[q]
        keep_maps[first + q, 0] = identity if f is None else f[:B]
        keep[first + q, 0] = nothing if f is None else f[B:]
        keep_maps[first + q, 1] = identity if u is None else u[B + width :]
        keep_maps[first + q, 2] = none if u is None else u[:B]
        keep[first + q, 1] = nothing if u is None else u[B : B + width]


def row_solve(maps_hbm, bg_ref, out_ref, xyz_ref, own_ref, maps_ref, sems, keep_maps, keep):
    width = bg_ref.shape[2]
    quads = [pl.ds(8 * h, 8) for h in range(4)]
    copies = start_copies([maps_hbm.at[q] for q in quads], [maps_ref.at[q] for q in quads], sems)
    quad_maps, quad_sides = [], []
    for h in range(4):
        copies[h].wait()
        maps, sides = [], []
        for p in range(4 * h, 4 * h + 4):
            part = [
                jnp.concatenate([maps_ref[2 * p, m], maps_ref[2 * p + 1, m]], axis=0) for m in range(5)
            ]
            maps.append((part[:2], part[2:4], (part[4], None)))
            sides.append([bg_ref[p, m].astype(f32) for m in range(2)])
        quad, side, entering, leaving = compose(maps, sides)
        keep_entries(keep_maps, keep, 4 * h, entering, leaving, width)
        quad_maps.append([split(m) for m in quad])
        quad_sides.append(side)
    row, side, entering, leaving = compose(quad_maps, quad_sides)
    keep_entries(keep_maps, keep, 16, entering, leaving, width)
    sent = [part.astype(bf16) for part in row]
    sides = split(side[0]) + split(side[1])
    for n in range(out_ref.shape[0]):
        for m in range(3):
            out_ref[n, m * B : (m + 1) * B] = sent[m]
        for m in range(4):
            out_ref[n, 3 * B + m * width : 3 * B + (m + 1) * width] = sides[m]
    high, low = 16 + lax.axis_index("zh"), 4 * lax.axis_index("zh") + lax.axis_index("zl")
    x, y, z = (keep_maps[low, m] for m in range(3))
    f = mm(jnp.concatenate([keep_maps[high, 0], keep[high, 0]], axis=0), x)
    u = mm(jnp.concatenate([keep_maps[high, 2], keep_maps[high, 1], keep[high, 1]], axis=0), y)
    z = mm(jnp.concatenate([keep_maps[high, 0], keep[high, 0]], axis=0), z)
    xyz_ref[0] = f[:B]
    xyz_ref[1] = u[B : 2 * B]
    xyz_ref[2] = u[:B] + z[:B]
    own_ref[0] = f[B:] + keep[low, 0]
    own_ref[1] = u[2 * B :] + z[B:] + keep[low, 1]


def chain(maps, bgs, keep):
    count = len(maps)
    f = bgs[0][0]
    entering = [None, f]
    for q in range(1, count - 1):
        f = mm(f, maps[q][0]) + bgs[q][0]
        entering.append(f)
    turned = [None] + [mm(entering[q], maps[q][2]) + bgs[q][1] for q in range(1, count)]
    keep[0, 0] = jnp.zeros_like(f)
    keep[count - 1, 1] = jnp.zeros_like(f)
    for q in range(1, count):
        keep[q, 0] = entering[q]
    u = turned[-1]
    for q in reversed(range(count - 1)):
        keep[q, 1] = u
        if q > 0:
            u = mm(u, maps[q][1]) + turned[q]


def top_solve(got_ref, xyz_ref, own_ref, wy_ref, local_ref, sep_ref, low_ref, keep):
    width = own_ref.shape[1]
    count = got_ref.shape[0]
    maps, bgs = [], []
    for q in range(count):
        maps.append([got_ref[q, m * B : (m + 1) * B].astype(f32) for m in range(3)])
        side = [
            got_ref[q, 3 * B + m * width : 3 * B + (m + 1) * width].astype(f32) for m in range(4)
        ]
        bgs.append([side[0] + side[1], side[2] + side[3]])
    chain(maps, bgs, keep)
    f, u = keep[lax.axis_index("row"), 0], keep[lax.axis_index("row"), 1]
    f, u = (
        mm(f, xyz_ref[0]) + own_ref[0],
        mm(u, xyz_ref[1]) + mm(f, xyz_ref[2]) + own_ref[1],
    )
    reached = mm(jnp.concatenate([f, u], axis=1), wy_ref[...])
    for s in range(4):
        value = local_ref[s] + reached[:, s * B : (s + 1) * B]
        sep_ref[s] = value
        low = value.astype(bf16)
        for n in range(low_ref.shape[0]):
            low_ref[n, s] = low


def join_upper(upper_ref, inv_ref, out_ref):
    for k in range(2):
        for i in range(4):
            out_ref[k, i * B : (i + 1) * B] = upper_ref[k, i].astype(f32).T.astype(bf16)
        out_ref[k, 4 * B :] = inv_ref[k].astype(f32).T.astype(bf16)


def leaf_backward(place_ref, solved_ref, forward_ref, upper_ref, out_ref):
    for j in range(out_ref.shape[0]):
        for k in range(2):
            solved = [solved_ref[place_ref[j, 4 * k + i]] for i in range(4)]
            total = dot(jnp.concatenate(solved, axis=1), upper_ref[j, k, : 4 * B])
            residual = (forward_ref[j, k].astype(f32) - total).astype(bf16)
            out_ref[j, k] = dot(residual, upper_ref[j, k, 4 * B :]).astype(bf16)


def turn_leaf(got_ref, out_ref):
    width = got_ref.shape[2]
    for k in range(2):
        whole = jnp.concatenate([got_ref[j, k] for j in range(got_ref.shape[0])], axis=0)
        out_ref[k] = whole.astype(f32).T.astype(bf16)


def turn_sep(place_ref, got_ref, out_ref, pass_ref):
    pass_ref[...] = place_ref[...]
    for k in range(2):
        s = 2 * lax.axis_index("core") + k
        whole = jnp.concatenate([got_ref[j, s] for j in range(got_ref.shape[0])], axis=0)
        out_ref[k] = whole.T


def exchange(value, axes):
    return lax.all_to_all(value, axes, split_axis=0, concat_axis=0, tiled=True)


def on_device(
    leaf_rhs,
    leaf_lower_inv,
    leaf_upper_inv,
    leaf_lower,
    leaf_upper,
    targets,
    sep_rhs,
    sep_lower_inv,
    sep_upper_inv,
    sep_lower_link,
    sep_upper_link,
):
    across = ("layer", "core")
    layers, rows = lax.axis_size("layer"), lax.axis_size("row")
    highs, lows = lax.axis_size("zh"), lax.axis_size("zl")
    groups = 2 * layers
    width = 256 // groups
    chips = highs * lows

    along = ("zh", "zl")
    pair = (2, width, B)

    sources = (sep_lower_inv, sep_lower_link, sep_upper_inv, sep_upper_link, sep_rhs)
    blocks = shaped((2, 4 * B + width, B), f32)
    half_maps = shaped((5, B // 2, B), bf16)
    maps = shaped((3, B, B), f32)
    mine, others = call(
        sep_prepare,
        (blocks, blocks),
        landing(sources) + [pltpu.VMEM((2, 256, B), f32)],
        "sep_prepare",
        hbm=range(0, 5),
        limit=VMEM_ALL,
    )(*sources)
    theirs = lax.ppermute(others, "core", [(0, 1), (1, 0)])

    sources = (leaf_rhs, leaf_lower_inv, leaf_lower)
    sent = call(
        leaf_forward,
        shaped((groups, 10 * width + 16, B), bf16),
        landing(sources),
        "leaf_forward",
        smem=(0,),
        hbm=(1, 2, 3),
        limit=VMEM_ALL,
        after=(mine,),
    )(targets, *sources)
    half = call(
        chip_maps,
        half_maps,
        [pltpu.VMEM((5, B, B), bf16), pltpu.VMEM((2, 2, 4 * B + width, B), f32)],
        "chip_maps",
        limit=VMEM_ALL,
        after=(sent,),
    )(mine, theirs)
    wy = call(
        chip_entries,
        shaped((2 * B, 4 * B), f32),
        [pltpu.VMEM((2, 2, 4 * B + width, B), f32)],
        "chip_entries",
        limit=VMEM_ALL,
    )(mine, theirs, half)
    by_chip = lax.all_gather(half, along + ("core",)).reshape((2 * chips,) + half_maps.shape)

    got = exchange(sent, across)
    place = got[:, 10 * width, :8].astype(jnp.int32)
    sums, forward = call(
        scatter_updates,
        (shaped((chips, 4, width, B), bf16), shaped((groups, 2, width, B), bf16)),
        [pltpu.VMEM((4 * chips, width, B), f32)],
        "scatter_updates",
        smem=(0,),
    )(place, got)

    bg, local = call(
        chip_solve,
        (shaped((chips,) + pair, bf16), shaped((4, width, B), f32)),
        [pltpu.VMEM((2, 2, 4 * B + width, B), f32)],
        "chip_solve",
    )(exchange(sums, along), mine, theirs)
    sent_on, xyz, own = call(
        row_solve,
        (shaped((rows, 3 * B + 4 * width, B), bf16), maps, shaped(pair, f32)),
        [
            pltpu.VMEM((2 * chips,) + half_maps.shape, bf16),
            pltpu.SemaphoreType.DMA((4,)),
            pltpu.VMEM((20, 3, B, B), f32),
            pltpu.VMEM((20,) + pair, f32),
        ],
        "row_solve",
        hbm=(0,),
        limit=VMEM_ALL,
    )(by_chip, exchange(bg, along))
    solved, solved_low = call(
        top_solve,
        (shaped((4, width, B), f32), shaped((chips, 4, width, B), bf16)),
        [pltpu.VMEM((rows,) + pair, f32)],
        "top_solve",
        limit=VMEM_ALL,
    )(exchange(sent_on, "row"), xyz, own, wy, local)

    joined = call(
        join_upper, shaped((2, 5 * B, B), bf16), name="join_upper", after=(sums,), limit=VMEM_ALL
    )(leaf_upper, leaf_upper_inv)
    upper = lax.all_gather(joined, across).reshape((groups, 2, 5 * B, B))
    low = exchange(solved_low, along).reshape(4 * chips, width, B)
    sep_all = lax.all_gather(solved, across).reshape((groups, 4, width, B))
    sep_part, place = call(
        turn_sep,
        (shaped((2, B, 256), f32), shaped(place.shape, jnp.int32)),
        name="turn_sep",
        after=(upper,),
    )(place, sep_all)
    back = call(
        leaf_backward,
        shaped((groups, 2, width, B), bf16),
        name="leaf_backward",
        smem=(0,),
    )(place, low, forward, upper)
    leaf_part = call(turn_leaf, shaped((2, B, 256), bf16), name="turn_leaf")(exchange(back, across))
    return (leaf_part, sep_part)


def solution(mesh):
    layers, rows, cols = (mesh.shape[name] for name in ("layer", "row", "col"))
    lows = 4
    fine = Mesh(
        mesh.devices.reshape(layers, rows, cols // (2 * lows), lows, 2),
        ("layer", "row", "zh", "zl", "core"),
    )
    leaf = ("layer", "row", "zh", "zl", "core")
    sep = ("row", "zh", "zl", "core")
    return jax.shard_map(
        on_device,
        mesh=fine,
        in_specs=(P(leaf),) * 6 + (P(sep),) * 5,
        out_specs=(P(leaf), P(sep)),
        check_vma=False,
    )
```
